256 devices in a mesh: blk: 64 (over y, z, x_hi), split: 4 (over x_lo, core).
Axes of the slice: x: 4 (x_hi: 2, x_lo: 2; x = x_hi * 2 + x_lo), y: 4, z: 8, core: 2. Of those that a mesh axis runs over, the one named last changes fastest.
Arguments:
- points: float32 [32, 262144], P(None, ('blk', 'split')), may hold values from -6 to 6
- vectors: float32 [16, 262144], P(None, ('blk', 'split')), may hold values from -6 to 6
- inv_length: float32 [32], replicated, may hold values from 0.05 to 0.3
- noise: float32 [262144], P(('blk', 'split')), may hold values from 0.5 to 2
Outputs:
- product: float32 [16, 262144], P(None, ('blk', 'split'))
The draws below stay inside these ranges and needn't reach their ends.
All inputs are finite; a program needn't handle non-finite values.
Results may differ from the reference program's by a relative error of at most 0.0003.
Values sent between devices are 32-bit elements; how exact they have to be, the bound alone decides.
No kernel may reach another device: no remote copies, remote signals or barrier semaphores. Data moves between devices by JAX's collectives and lax.ppermute only.
A program may use at most 64 MiB of HBM per device.

```python
import math
import jax
import jax.numpy as jnp
from jax import lax

DIMS = 32
RHS = 16
SHIFTS = 2
BLOCK = 4096
N = 262144
N_BLK = 64


def block_scale(stream_key, dims, cuts, low, high):
    def one(position, shards_of):
        draws = jax.random.uniform(jax.random.fold_in(jax.random.fold_in(stream_key, 6), position), (shards_of,), jnp.float32, low / len(cuts), high / len(cuts))
        return jnp.repeat(jnp.exp(draws), dims[position] // shards_of).reshape((-1,) + (1,) * (len(dims) - position - 1))

    level = one(*cuts[0])
    for cut in cuts[1:]:
        level = level * one(*cut)
    return level


def normal_values(own_key, extent, deviation, limit, split=(), kind=jnp.bfloat16):
    drawn = deviation * jax.random.normal(own_key, extent, jnp.float32)
    if split:
        drawn = drawn * block_scale(own_key, extent, split, -0.22, 0.18)
    return jnp.clip(drawn, -limit, limit).astype(kind)


def setup_inputs(seed: int = 0) -> dict:
    arg_keys = jax.random.split(jax.random.key(seed), 5)
    points = normal_values(arg_keys[0], (DIMS, N), 1.0, 6.0, ((1, 256),), jnp.float32)
    vectors = normal_values(arg_keys[1], (RHS, N), 1.0, 6.0, ((1, 256),), jnp.float32)
    inv_length = jnp.clip(jnp.exp(jax.random.uniform(arg_keys[2], (DIMS,), jnp.float32, math.log(0.05), math.log(0.3))), 0.05, 0.3)
    noise = jnp.clip(0.5 + 1.5 * jax.random.uniform(arg_keys[3], (N,), jnp.float32) ** block_scale(arg_keys[3], (N,), ((0, 256),), -0.2, 0.2), 0.5, 2.0)
    return dict(points=points, vectors=vectors, inv_length=inv_length, noise=noise)


SIGNAL = 0.03125
ROOT_FIVE = 2.23606797749979

def matern(rows, cols):
    row_sq = lax.optimization_barrier(jnp.sum(rows * rows, axis=0))
    col_sq = lax.optimization_barrier(jnp.sum(cols * cols, axis=0))
    cross = lax.dot_general(rows, cols, (((0,), (0,)), ((), ())), precision=lax.Precision.HIGHEST, preferred_element_type=jnp.float32)
    dist_sq = jnp.maximum(row_sq[:, None] + col_sq[None, :] - 2.0 * cross, 0.0)
    radius = jnp.sqrt(dist_sq)
    return SIGNAL * (1.0 + ROOT_FIVE * radius + 5.0 / 3.0 * dist_sq) * jnp.exp(-ROOT_FIVE * radius)

def reference(points, vectors, inv_length, noise):
    scaled = points * inv_length[:, None]
    width = SHIFTS * BLOCK
    ext_points = jnp.concatenate([scaled[:, N - width:], scaled, scaled[:, :width]], axis=1)
    ext_vectors = jnp.concatenate([vectors[:, N - width:], vectors, vectors[:, :width]], axis=1)
    span = (2 * SHIFTS + 1) * BLOCK

    def one_block(index):
        start = (index * BLOCK).astype(jnp.int32)
        rows = lax.dynamic_slice_in_dim(scaled, start, BLOCK, 1)
        cols = lax.dynamic_slice_in_dim(ext_points, start, span, 1)
        col_vec = lax.dynamic_slice_in_dim(ext_vectors, start, span, 1)
        tile = matern(rows, cols)
        return lax.dot_general(col_vec, tile, (((1,), (1,)), ((), ())), precision=lax.Precision.HIGHEST, preferred_element_type=jnp.float32)
    blocks = lax.map(one_block, jnp.arange(N_BLK, dtype=jnp.int32))
    result = jnp.transpose(blocks, (1, 0, 2)).reshape(RHS, N)
    return result + noise[None, :] * vectors
```

```python
import functools

import jax
import jax.numpy as jnp
from jax import lax
from jax.experimental import pallas as pl
from jax.experimental.pallas import tpu as pltpu
from jax.sharding import PartitionSpec as P

SIGNAL = 0.03125
ROOT_FIVE = 2.23606797749979
LOG2E = 1.4426950408889634
POINT_SCALE = ROOT_FIVE * LOG2E
OUT_SCALE = SIGNAL / (3.0 * LOG2E * LOG2E)
DIMS = 32
RHS = 16
DEPTH = 256
CHUNK = 512
BF16 = jnp.bfloat16
F32 = jnp.float32


def dot(a, b, ca, cb):
    return lax.dot_general(a, b, (((ca,), (cb,)), ((), ())), preferred_element_type=F32)


def pieces(x):
    hi = x.astype(BF16)
    rest = x - hi.astype(F32)
    mid = rest.astype(BF16)
    lo = (rest - mid.astype(F32)).astype(BF16)
    return hi, mid, lo


def norm_rows(sq, first):
    s1, s2, s3 = (p.astype(F32) for p in pieces(sq))
    row = lax.broadcasted_iota(jnp.int32, (16, sq.shape[1]), 0)
    out = jnp.where(row < 6, 1.0, 0.0)
    for k, s in enumerate((s1, s2, s3)):
        out = jnp.where(row == first + k, s, out)
    return out.astype(BF16)


def features(points, inv_length, rows):
    x = (points * inv_length) * POINT_SCALE
    sq = jnp.sum(x * x, axis=0, keepdims=True)
    hi, mid, lo = pieces(x)
    pad = jnp.zeros((DEPTH - 208, x.shape[1]), BF16)
    if rows:
        two = jnp.asarray(-2.0, BF16)
        hi, mid, lo = hi * two, mid * two, lo * two
        return jnp.concatenate([hi, mid, hi, lo, mid, hi, norm_rows(sq, 0), pad], axis=0)
    return jnp.concatenate([hi, hi, mid, hi, mid, lo, norm_rows(sq, 3), pad], axis=0)


def halves(v):
    hi = v.astype(BF16)
    return jnp.concatenate([hi, (v - hi.astype(F32)).astype(BF16)], axis=0)


def kernel_tile(dist_sq):
    b2 = jnp.maximum(dist_sq, 1e-30)
    b = b2 * lax.rsqrt(b2)
    t = ((b + 3.0 * LOG2E) * b + 3.0 * LOG2E * LOG2E) * jnp.exp2(-b)
    hi = t.astype(BF16)
    return hi, (t - hi.astype(F32)).astype(BF16)


def fold(x):
    return (x[:RHS] + x[RHS:]) * OUT_SCALE


def prep_kernel(count, *refs):
    inv = refs[count][...]
    at_ref, vr_ref = refs[count + 1 :]
    for k in range(count):
        x = refs[k]
        width = x.shape[1]
        f = features(x[:DIMS, :], inv, True)
        at_ref[k * width : (k + 1) * width, :] = f.T
        vr_ref[:, k * width : (k + 1) * width] = halves(x[DIMS:, :])


def tile_kernel(both, at_ref, vr_ref, x_ref, inv_ref, *rest):
    if both:
        fwd_ref, bwd_ref, b_ref, vc_ref, acc_ref = rest
    else:
        bwd_ref, b_ref, vc_ref, acc_ref = rest
    b_ref[...] = features(x_ref[:DIMS, :], inv_ref[...], False)
    vc_ref[...] = halves(x_ref[DIMS:, :])
    acc_ref[...] = jnp.zeros_like(acc_ref)

    def step(i, carry):
        rows = pl.ds(pl.multiple_of(i * CHUNK, CHUNK), CHUNK)
        hi, lo = kernel_tile(dot(at_ref[rows, :], b_ref[...], 1, 0))
        vr = vr_ref[:, rows]
        acc_ref[...] += dot(vr, hi, 1, 0) + dot(vr, lo, 1, 0)
        if both:
            vc = vc_ref[...]
            fwd_ref[:, rows] = fold(dot(vc, hi, 1, 1) + dot(vc, lo, 1, 1))
        return carry

    lax.fori_loop(0, at_ref.shape[0] // CHUNK, step, 0)
    bwd_ref[...] = fold(acc_ref[...])


VMEM = pl.BlockSpec(memory_space=pltpu.VMEM)
PARAMS = pltpu.CompilerParams(vmem_limit_bytes=40 * 2**20)


def prep(xs, inv):
    width = xs[0].shape[1]
    n = len(xs) * width
    return pl.pallas_call(
        functools.partial(prep_kernel, len(xs)),
        out_shape=(
            jax.ShapeDtypeStruct((n, DEPTH), BF16),
            jax.ShapeDtypeStruct((2 * RHS, n), BF16),
        ),
        in_specs=[VMEM] * (len(xs) + 1),
        out_specs=(VMEM, VMEM),
        compiler_params=PARAMS,
        cost_estimate=pl.CostEstimate(flops=n * 2000, bytes_accessed=n * 800, transcendentals=0),
        name="prep",
    )(*xs, inv)


def tiles(at, vr, x, inv, both):
    n, width = at.shape[0], x.shape[1]
    bwd = jax.ShapeDtypeStruct((RHS, width), F32)
    fwd = jax.ShapeDtypeStruct((RHS, n), F32)
    return pl.pallas_call(
        functools.partial(tile_kernel, both),
        out_shape=(fwd, bwd) if both else bwd,
        in_specs=[VMEM] * 4,
        out_specs=(VMEM, VMEM) if both else VMEM,
        scratch_shapes=[
            pltpu.VMEM((DEPTH, width), BF16),
            pltpu.VMEM((2 * RHS, width), BF16),
            pltpu.VMEM((2 * RHS, width), F32),
        ],
        compiler_params=PARAMS,
        cost_estimate=pl.CostEstimate(
            flops=n * width * 2 * DEPTH * (5 if both else 3), bytes_accessed=n * 600, transcendentals=2 * n * width
        ),
        name="both" if both else "own",
    )(at, vr, x, inv)


def shifted(value, steps):
    count = lax.axis_size("blk")
    return lax.ppermute(value, "blk", [(s, (s + steps) % count) for s in range(count)])


def swapped(value, mask):
    count = lax.axis_size("split")
    return lax.ppermute(value, "split", [(s, s ^ mask) for s in range(count)])


def body(points, vectors, inv_length, noise):
    inv = inv_length[:, None]
    own = jnp.concatenate([points, vectors], axis=0)
    far = swapped(own, 2)
    two = shifted(own, 2)
    one = shifted(own, 1)
    at0, vr0 = prep([own], inv)
    total = tiles(at0, vr0, own, inv, False)
    near = swapped(jnp.concatenate([own, far], axis=1), 1)
    width = own.shape[1]
    at2, vr2 = prep([far], inv)
    ata, vra = jnp.concatenate([at0, at2], axis=0), jnp.concatenate([vr0, vr2], axis=1)
    fwd_a2, ret_a2 = tiles(ata, vra, two, inv, True)
    atb, vrb = prep([near], inv)
    fwd_b2, ret_b2 = tiles(atb, vrb, two, inv, True)
    back2 = shifted(ret_a2 + ret_b2, -2)
    fwd_b1, ret_b1 = tiles(atb, vrb, one, inv, True)
    give_near = swapped(fwd_b2 + fwd_b1, 1)
    fwd_a1, ret_a1 = tiles(ata, vra, one, inv, True)
    back1 = shifted(ret_a1 + ret_b1, -1)
    rows = fwd_a2 + fwd_a1 + give_near
    give_far = swapped(rows[:, width:], 2)
    total = total + tiles(atb, vrb, own, inv, False) + tiles(at2, vr2, own, inv, False)
    return total + rows[:, :width] + give_far + back1 + back2 + noise[None, :] * vectors


def solution(mesh):
    placed = (P(None, ("blk", "split")), P(None, ("blk", "split")), P(), P(("blk", "split")))
    return jax.shard_map(
        body, mesh=mesh, in_specs=placed, out_specs=P(None, ("blk", "split")), check_vma=False
    )
```

```python
import functools

import jax
import jax.numpy as jnp
from jax import lax
from jax.experimental import pallas as pl
from jax.experimental.pallas import tpu as pltpu
from jax.sharding import PartitionSpec as P

SIGNAL = 0.03125
ROOT_FIVE = 2.23606797749979
LOG2E = 1.4426950408889634
POINT_SCALE = ROOT_FIVE * LOG2E
SHIFT = 1.5 * LOG2E
FLOOR = 0.75 * LOG2E * LOG2E
OUT_SCALE = SIGNAL / (3.0 * LOG2E * LOG2E) * 2.0**SHIFT
DIMS = 32
RHS = 16
DEPTH = 256
TILE = 256
STEP_TILES = 16
BF16 = jnp.bfloat16
F32 = jnp.float32
LOW = jnp.bfloat16


def dot(a, b, ca, cb):
    return lax.dot_general(a, b, (((ca,), (cb,)), ((), ())), preferred_element_type=F32)


def pieces(x):
    hi = x.astype(BF16)
    rest = x - hi.astype(F32)
    mid = rest.astype(BF16)
    lo = (rest - mid.astype(F32)).astype(BF16)
    return hi, mid, lo


def norm_rows(sq, first):
    s1, s2, s3 = (p.astype(F32) for p in pieces(sq))
    row = lax.broadcasted_iota(jnp.int32, (16, sq.shape[1]), 0)
    out = jnp.where(row < 6, 1.0, 0.0)
    for k, s in enumerate((s1, s2, s3)):
        out = jnp.where(row == first + k, s, out)
    return out.astype(BF16)


def features(points, inv_length, rows):
    x = (points * inv_length) * POINT_SCALE
    sq = jnp.sum(x * x, axis=0, keepdims=True)
    hi, mid, lo = pieces(x)
    pad = jnp.zeros((DEPTH - 208, x.shape[1]), BF16)
    if rows:
        two = jnp.asarray(-2.0, BF16)
        hi, mid, lo = hi * two, mid * two, lo * two
        return jnp.concatenate([hi, mid, hi, lo, mid, hi, norm_rows(sq, 0), pad], axis=0)
    return jnp.concatenate([hi, hi, mid, hi, mid, lo, norm_rows(sq, 3), pad], axis=0)


def halves(v, kind):
    hi = v.astype(kind)
    return jnp.concatenate([hi, (v - hi.astype(F32)).astype(kind)], axis=0)


def kernel_tile(dist_sq):
    b2 = jnp.maximum(dist_sq, 1e-30)
    w = -SHIFT - b2 * lax.rsqrt(b2)
    t = (w * w + FLOOR) * jnp.exp2(w)
    hi = t.astype(BF16)
    return hi, (t - hi.astype(F32)).astype(LOW)


def fold(x):
    return (x[:RHS] + x[RHS:]) * OUT_SCALE


def prep_kernel(count, *refs):
    inv = refs[count][...]
    at_ref, v_ref = refs[count + 1 : count + 3]
    for k in range(count):
        x = refs[k]
        width = x.shape[1]
        at_ref[k * width : (k + 1) * width, :] = features(x[:DIMS, :], inv, True).T
        v_ref[:, k * width : (k + 1) * width] = x[DIMS:, :]


def first_kernel(points_ref, vectors_ref, inv_ref, x_ref, at_ref):
    points = points_ref[...]
    x_ref[:DIMS, :] = points
    x_ref[DIMS:, :] = vectors_ref[...]
    at_ref[...] = features(points, inv_ref[...], True).T


def tile_kernel(both, count, at_ref, v_ref, inv_ref, *rest):
    xs = rest[:count]
    if both:
        fwd_ref, bwd_ref, b_ref, vr_ref, vc_ref, facc_ref, acc_ref, d_ref, hi_ref, lo_ref = rest[count:]
    else:
        bwd_ref, b_ref, vr_ref, acc_ref, d_ref, hi_ref, lo_ref = rest[count:]
    rows = at_ref.shape[0]
    for k, x in enumerate(xs):
        width = x.shape[1]
        cols = slice(k * width, (k + 1) * width)
        b_ref[:, cols] = features(x[:DIMS, :], inv_ref[...], False)
        if both:
            vc_ref[:, cols] = halves(x[DIMS:, :], BF16)
    vr_ref[...] = halves(v_ref[...], BF16)
    acc_ref[...] = jnp.zeros_like(acc_ref)
    if both:
        facc_ref[...] = jnp.zeros_like(facc_ref)
    across = count * width // TILE
    down = STEP_TILES // across
    chunks = rows // TILE

    def span(i):
        return pl.ds(pl.multiple_of(i * TILE, TILE), TILE)

    def distances(i, j):
        return dot(at_ref[span(i), :], b_ref[:, j * TILE : (j + 1) * TILE], 1, 0)

    def products(hi, lo, i, j):
        cols = slice(j * TILE, (j + 1) * TILE)
        vr = vr_ref[:, span(i)]
        acc_ref[:, cols] += dot(vr, hi, 1, 0) + dot(vr, lo, 1, 0)
        if both:
            vc = vc_ref[:, cols]
            facc_ref[:, span(i)] += dot(vc, hi, 1, 1) + dot(vc, lo, 1, 1)

    hi_ref[...] = jnp.zeros_like(hi_ref)
    lo_ref[...] = jnp.zeros_like(lo_ref)
    d_ref[...] = distances(0, 0)

    def step(k, carry):
        now, hi, lo = d_ref[...], hi_ref[...], lo_ref[...]
        i, j = jnp.maximum(k * down - 1, 0), across - 1
        for t in range(STEP_TILES):
            ahead = k * down + (t + 1) // across
            if t == STEP_TILES - 1:
                ahead = jnp.where(ahead < chunks, ahead, 0)
            later = distances(ahead, (t + 1) % across)
            products(hi, lo, i, j)
            hi, lo = kernel_tile(now)
            now, i, j = later, k * down + t // across, t % across
        d_ref[...], hi_ref[...], lo_ref[...] = now, hi, lo
        return carry

    lax.fori_loop(0, chunks // down, step, 0)
    products(hi_ref[...], lo_ref[...], chunks - 1, across - 1)
    bwd_ref[...] = fold(acc_ref[...])
    if both:
        fwd_ref[...] = fold(facc_ref[...])


VMEM = pl.BlockSpec(memory_space=pltpu.VMEM)
PARAMS = pltpu.CompilerParams(vmem_limit_bytes=40 * 2**20)


def first(points, vectors, inv):
    width = points.shape[1]
    return pl.pallas_call(
        first_kernel,
        out_shape=(
            jax.ShapeDtypeStruct((DIMS + RHS, width), F32),
            jax.ShapeDtypeStruct((width, DEPTH), BF16),
        ),
        in_specs=[VMEM] * 3,
        out_specs=(VMEM, VMEM),
        compiler_params=PARAMS,
        cost_estimate=pl.CostEstimate(flops=width * 2000, bytes_accessed=width * 800, transcendentals=0),
        name="first",
    )(points, vectors, inv)


def prep(xs, inv):
    width = xs[0].shape[1]
    n = len(xs) * width
    return pl.pallas_call(
        functools.partial(prep_kernel, len(xs)),
        out_shape=(
            jax.ShapeDtypeStruct((n, DEPTH), BF16),
            jax.ShapeDtypeStruct((RHS, n), F32),
        ),
        in_specs=[VMEM] * (len(xs) + 1),
        out_specs=(VMEM, VMEM),
        compiler_params=PARAMS,
        cost_estimate=pl.CostEstimate(flops=n * 2000, bytes_accessed=n * 800, transcendentals=0),
        name="prep",
    )(*xs, inv)


def tiles(at, v, inv, xs, both):
    n, width = at.shape[0], len(xs) * xs[0].shape[1]
    bwd = jax.ShapeDtypeStruct((RHS, width), F32)
    fwd = jax.ShapeDtypeStruct((RHS, n), F32)
    across = [pltpu.VMEM((2 * RHS, width), BF16)] if both else []
    total = [pltpu.VMEM((2 * RHS, n), F32)] if both else []
    return pl.pallas_call(
        functools.partial(tile_kernel, both, len(xs)),
        out_shape=(fwd, bwd) if both else bwd,
        in_specs=[VMEM] * (3 + len(xs)),
        out_specs=(VMEM, VMEM) if both else VMEM,
        scratch_shapes=[pltpu.VMEM((DEPTH, width), BF16), pltpu.VMEM((2 * RHS, n), BF16)]
        + across
        + total
        + [
            pltpu.VMEM((2 * RHS, width), F32),
            pltpu.VMEM((TILE, TILE), F32),
            pltpu.VMEM((TILE, TILE), BF16),
            pltpu.VMEM((TILE, TILE), LOW),
        ],
        compiler_params=PARAMS,
        cost_estimate=pl.CostEstimate(
            flops=n * width * 2 * DEPTH * (5 if both else 3), bytes_accessed=n * 600, transcendentals=2 * n * width
        ),
        name="both" if both else "own",
    )(at, v, inv, *xs)


def shifted(value, steps):
    count = lax.axis_size("blk")
    return lax.ppermute(value, "blk", [(s, (s + steps) % count) for s in range(count)])


def swapped(value, mask):
    count = lax.axis_size("split")
    return lax.ppermute(value, "split", [(s, s ^ mask) for s in range(count)])


def body(points, vectors, inv_length, noise):
    inv = inv_length[:, None]
    own, at0 = first(points, vectors, inv)
    far = swapped(own, 2)
    two = shifted(own, 2)
    one = shifted(own, 1)
    total = tiles(at0, vectors, inv, [own], False)
    near = swapped(jnp.concatenate([own, far], axis=1), 1)
    width = own.shape[1]
    at2, v2 = prep([far], inv)
    ata, va = jnp.concatenate([at0, at2], axis=0), jnp.concatenate([vectors, v2], axis=1)
    fwd_a, ret_a = tiles(ata, va, inv, [two, one], True)
    atb, vb = prep([near], inv)
    fwd_b, ret_b = tiles(atb, vb, inv, [two, one], True)
    give_near = swapped(fwd_b, 1)
    ret = ret_a + ret_b
    back2 = shifted(ret[:, :width], -2)
    back1 = shifted(ret[:, width:], -1)
    rows = fwd_a + give_near
    give_far = swapped(rows[:, width:], 2)
    total = total + tiles(atb, vb, inv, [own], False) + tiles(at2, v2, inv, [own], False)
    return total + rows[:, :width] + give_far + back1 + back2 + noise[None, :] * vectors


def solution(mesh):
    placed = (P(None, ("blk", "split")), P(None, ("blk", "split")), P(), P(("blk", "split")))
    return jax.shard_map(
        body, mesh=mesh, in_specs=placed, out_specs=P(None, ("blk", "split")), check_vma=False
    )
```

```python
import functools

import jax
import jax.numpy as jnp
from jax import lax
from jax.experimental import pallas as pl
from jax.experimental.pallas import tpu as pltpu
from jax.sharding import PartitionSpec as P

SIGNAL = 0.03125
ROOT_FIVE = 2.23606797749979
LOG2E = 1.4426950408889634
POINT_SCALE = ROOT_FIVE * LOG2E
SHIFT = 1.5 * LOG2E
FLOOR = 0.75 * LOG2E * LOG2E
OUT_SCALE = SIGNAL / (3.0 * LOG2E * LOG2E) * 2.0**SHIFT
DIMS = 32
RHS = 16
DEPTH = 256
TILE = 256
GROUP = 2
STEP_TILES = 32
BF16 = jnp.bfloat16
F32 = jnp.float32
LOW = jnp.bfloat16


def dot(a, b, ca, cb):
    return lax.dot_general(a, b, (((ca,), (cb,)), ((), ())), preferred_element_type=F32)


def pieces(x):
    hi = x.astype(BF16)
    rest = x - hi.astype(F32)
    mid = rest.astype(BF16)
    lo = (rest - mid.astype(F32)).astype(BF16)
    return hi, mid, lo


def norm_rows(sq, first):
    s1, s2, s3 = (p.astype(F32) for p in pieces(sq))
    row = lax.broadcasted_iota(jnp.int32, (16, sq.shape[1]), 0)
    out = jnp.where(row < 6, 1.0, 0.0)
    for k, s in enumerate((s1, s2, s3)):
        out = jnp.where(row == first + k, s, out)
    return out.astype(BF16)


def features(x, rows):
    sq = jnp.sum(x * x, axis=0, keepdims=True)
    hi, mid, lo = pieces(x)
    pad = jnp.zeros((DEPTH - 208, x.shape[1]), BF16)
    if rows:
        two = jnp.asarray(-2.0, BF16)
        hi, mid, lo = hi * two, mid * two, lo * two
        return jnp.concatenate([hi, mid, hi, lo, mid, hi, norm_rows(sq, 0), pad], axis=0)
    return jnp.concatenate([hi, hi, mid, hi, mid, lo, norm_rows(sq, 3), pad], axis=0)


def halves(v, kind):
    hi = v.astype(kind)
    return jnp.concatenate([hi, (v - hi.astype(F32)).astype(kind)], axis=0)


def kernel_tile(b2):
    w = -SHIFT - b2 * lax.rsqrt(b2)
    t = (w * w + FLOOR) * jnp.exp2(w)
    hi = t.astype(BF16)
    return hi, (t - hi.astype(F32)).astype(LOW)


def fold(x):
    return (x[:RHS] + x[RHS:]) * OUT_SCALE


def first_kernel(x_ref, at_ref, b_ref):
    x = x_ref[:DIMS, :]
    at_ref[...] = features(x, True).T
    b_ref[...] = features(x, False)


def rows_kernel(x_ref, at_ref):
    at_ref[...] = features(x_ref[:DIMS, :], True).T


def cols_kernel(x_ref, b_ref):
    b_ref[...] = features(x_ref[:DIMS, :], False)


def tile_kernel(both, at_ref, v_ref, b_ref, *rest):
    if both:
        x_ref, fwd_ref, bwd_ref, vc_ref, facc_ref = rest[:5]
    else:
        bwd_ref = rest[0]
    vr_ref, acc_ref, even_ref, odd_ref, hi_ref, lo_ref, slot_ref = rest[5 if both else 1 :]
    across, groups = b_ref.shape[1] // TILE, at_ref.shape[0] // (TILE * GROUP)
    down = min(STEP_TILES // (GROUP * across), groups)
    slot_ref[0] = 0
    slot = slot_ref[0]
    if both:
        vc_ref[...] = halves(x_ref[DIMS:, :], BF16)
        facc_ref[...] = jnp.zeros_like(facc_ref)
    vr_ref[...] = halves(v_ref[DIMS:, :], BF16)
    acc_ref[...] = jnp.zeros_like(acc_ref)

    def distances(ref, i, j):
        rows = pl.ds(pl.multiple_of(i * TILE * GROUP, TILE * GROUP), TILE * GROUP)
        d2 = dot(at_ref[rows, :], b_ref[:, j * TILE : (j + 1) * TILE], 1, 0)
        ref[0] = jnp.maximum(d2, 1e-30)

    def products(hi, lo, i, j):
        cols = slice(j * TILE, (j + 1) * TILE)
        rows = pl.ds(pl.multiple_of(i * TILE, TILE), TILE)
        vr = vr_ref[:, rows]
        acc_ref[:, cols] += dot(vr, hi, 1, 0) + dot(vr, lo, 1, 0)
        if both:
            vc = vc_ref[:, cols]
            facc_ref[:, rows] += dot(vc, hi, 1, 1) + dot(vc, lo, 1, 1)

    hi_ref[...] = jnp.zeros_like(hi_ref)
    lo_ref[...] = jnp.zeros_like(lo_ref)
    distances(even_ref, 0, 0)

    def step(k, carry):
        hi, lo = hi_ref[...], lo_ref[...]
        i, j = jnp.maximum(k * down * GROUP - 1, 0), across - 1
        for t in range(down * across):
            now, later = (even_ref, odd_ref) if t % 2 == 0 else (odd_ref, even_ref)
            ahead = k * down + (t + 1) // across
            if t == down * across - 1:
                ahead = jnp.where(ahead < groups, ahead, 0)
            distances(later, ahead, (t + 1) % across)
            for g in range(GROUP):
                products(hi, lo, i, j)
                hi, lo = kernel_tile(now[slot, g * TILE : (g + 1) * TILE, :])
                i, j = (k * down + t // across) * GROUP + g, t % across
        hi_ref[...], lo_ref[...] = hi, lo
        return carry

    lax.fori_loop(0, groups // down, step, 0)
    products(hi_ref[...], lo_ref[...], groups * GROUP - 1, across - 1)
    bwd_ref[...] = fold(acc_ref[...])
    if both:
        fwd_ref[...] = fold(facc_ref[...])


VMEM = pl.BlockSpec(memory_space=pltpu.VMEM)
PARAMS = pltpu.CompilerParams(vmem_limit_bytes=40 * 2**20)


def first(x):
    n = x.shape[1]
    return pl.pallas_call(
        first_kernel,
        out_shape=(jax.ShapeDtypeStruct((n, DEPTH), BF16), jax.ShapeDtypeStruct((DEPTH, n), BF16)),
        in_specs=[VMEM],
        out_specs=(VMEM, VMEM),
        compiler_params=PARAMS,
        cost_estimate=pl.CostEstimate(flops=n * 64, bytes_accessed=n * 16, transcendentals=0),
        name="first",
    )(x)


def prep(x, rows):
    n = x.shape[1]
    return pl.pallas_call(
        rows_kernel if rows else cols_kernel,
        out_shape=jax.ShapeDtypeStruct((n, DEPTH) if rows else (DEPTH, n), BF16),
        in_specs=[VMEM],
        out_specs=VMEM,
        compiler_params=PARAMS,
        cost_estimate=pl.CostEstimate(flops=n * 64, bytes_accessed=n * 16, transcendentals=0),
        name="rows" if rows else "cols",
    )(x)


def tiles(at, v, b, x=None):
    n, width = at.shape[0], b.shape[1]
    both = x is not None
    bwd = jax.ShapeDtypeStruct((RHS, width), F32)
    fwd = jax.ShapeDtypeStruct((RHS, n), F32)
    more = [pltpu.VMEM((2 * RHS, width), BF16), pltpu.VMEM((2 * RHS, n), F32)] if both else []
    return pl.pallas_call(
        functools.partial(tile_kernel, both),
        out_shape=(fwd, bwd) if both else bwd,
        in_specs=[VMEM] * (4 if both else 3),
        out_specs=(VMEM, VMEM) if both else VMEM,
        scratch_shapes=more
        + [
            pltpu.VMEM((2 * RHS, n), BF16),
            pltpu.VMEM((2 * RHS, width), F32),
            pltpu.VMEM((1, TILE * GROUP, TILE), F32),
            pltpu.VMEM((1, TILE * GROUP, TILE), F32),
            pltpu.VMEM((TILE, TILE), BF16),
            pltpu.VMEM((TILE, TILE), LOW),
            pltpu.SMEM((1,), jnp.int32),
        ],
        compiler_params=PARAMS,
        cost_estimate=pl.CostEstimate(
            flops=n * width * 8, bytes_accessed=n * 16, transcendentals=0
        ),
        name="both" if both else "own",
    )(at, v, b, *([x] if both else []))


def shifted(value, steps):
    count = lax.axis_size("blk")
    return lax.ppermute(value, "blk", [(s, (s + steps) % count) for s in range(count)])


def swapped(value, mask):
    count = lax.axis_size("split")
    return lax.ppermute(value, "split", [(s, s ^ mask) for s in range(count)])


def after(value, *others):
    return lax.optimization_barrier((value, *others))[0]


def body(points, vectors, inv_length, noise):
    own = jnp.concatenate([points * inv_length[:, None] * POINT_SCALE, vectors], axis=0)
    width = own.shape[1]
    far = swapped(own, 2)
    two = shifted(own, 2)
    at0, b0 = first(own)
    total = tiles(at0, own, b0)
    far = after(far, total)
    pair = jnp.concatenate([own, far], axis=1)
    other = swapped(pair, 1)
    one = shifted(after(own, far), 1)
    at1 = prep(far, True)
    total = total + tiles(at1, far, b0)
    other = after(other, total)
    at_other = prep(other, True)
    total = total + tiles(at_other, other, b0)
    block = jnp.concatenate([pair, other], axis=1)
    at_pair = jnp.concatenate([at0, at1], axis=0)
    at = jnp.concatenate([at_pair, at_other], axis=0)
    two = after(two, total)
    fwd2, ret2 = tiles(at, block, prep(two, False), two)
    back2 = shifted(ret2, -2)
    one = after(one, ret2)
    b1 = prep(one, False)
    fwd_other, ret_other = tiles(at_other, other, b1, one)
    give_near = swapped(fwd_other + fwd2[:, 2 * width :], 1)
    fwd_pair, ret_pair = tiles(at_pair, after(pair, ret_other), b1, one)
    back1 = shifted(ret_other + ret_pair, -1)
    rows = fwd_pair + fwd2[:, : 2 * width] + give_near
    give_far = swapped(rows[:, width:], 2)
    return total + rows[:, :width] + give_far + back1 + back2 + noise[None, :] * vectors


def solution(mesh):
    placed = (P(None, ("blk", "split")), P(None, ("blk", "split")), P(), P(("blk", "split")))
    return jax.shard_map(
        body, mesh=mesh, in_specs=placed, out_specs=P(None, ("blk", "split")), check_vma=False
    )
```

```python
import functools

import jax
import jax.numpy as jnp
from jax import lax
from jax.experimental import pallas as pl
from jax.experimental.pallas import tpu as pltpu
from jax.sharding import PartitionSpec as P

SIGNAL = 0.03125
ROOT_FIVE = 2.23606797749979
LOG2E = 1.4426950408889634
POINT_SCALE = ROOT_FIVE * LOG2E
SHIFT = 1.5 * LOG2E
FLOOR = 0.75 * LOG2E * LOG2E
OUT_SCALE = SIGNAL / (3.0 * LOG2E * LOG2E) * 2.0**SHIFT
DIMS = 32
RHS = 16
DEPTH = 256
TILE = 256
GROUP = 2
STEP_TILES = 32
BF16 = jnp.bfloat16
F32 = jnp.float32
LOW = jnp.bfloat16


def dot(a, b, ca, cb):
    return lax.dot_general(a, b, (((ca,), (cb,)), ((), ())), preferred_element_type=F32)


def pieces(x):
    hi = x.astype(BF16)
    rest = x - hi.astype(F32)
    mid = rest.astype(BF16)
    lo = (rest - mid.astype(F32)).astype(BF16)
    return hi, mid, lo


def norm_rows(sq, first):
    s1, s2, s3 = (p.astype(F32) for p in pieces(sq))
    row = lax.broadcasted_iota(jnp.int32, (16, sq.shape[1]), 0)
    out = jnp.where(row < 6, 1.0, 0.0)
    for k, s in enumerate((s1, s2, s3)):
        out = jnp.where(row == first + k, s, out)
    return out.astype(BF16)


def features(x, rows):
    sq = jnp.sum(x * x, axis=0, keepdims=True)
    hi, mid, lo = pieces(x)
    pad = jnp.zeros((DEPTH - 208, x.shape[1]), BF16)
    if rows:
        two = jnp.asarray(-2.0, BF16)
        hi, mid, lo = hi * two, mid * two, lo * two
        return jnp.concatenate([hi, mid, hi, lo, mid, hi, norm_rows(sq, 0), pad], axis=0)
    return jnp.concatenate([hi, hi, mid, hi, mid, lo, norm_rows(sq, 3), pad], axis=0)


def halves(v, kind):
    hi = v.astype(kind)
    return jnp.concatenate([hi, (v - hi.astype(F32)).astype(kind)], axis=0)


def kernel_tile(b2):
    w = -SHIFT - b2 * lax.rsqrt(b2)
    t = (w * w + FLOOR) * jnp.exp2(w)
    hi = t.astype(BF16)
    return hi, (t - hi.astype(F32)).astype(LOW)


def fold(x):
    return (x[:RHS] + x[RHS:]) * OUT_SCALE


def first_kernel(x_ref, at_ref, b_ref):
    x = x_ref[:DIMS, :]
    at_ref[...] = features(x, True).T
    b_ref[...] = features(x, False)


def rows_kernel(x_ref, at_ref):
    at_ref[...] = features(x_ref[:DIMS, :], True).T


def cols_kernel(x_ref, b_ref):
    b_ref[...] = features(x_ref[:DIMS, :], False)


def tile_kernel(both, start, count, at_ref, v_ref, b_ref, *rest):
    if both:
        x_ref, fwd_ref, bwd_ref, vc_ref, facc_ref = rest[:5]
    else:
        bwd_ref = rest[0]
    vr_ref, acc_ref, even_ref, odd_ref, hi_ref, lo_ref, slot_ref = rest[5 if both else 1 :]
    across, groups = b_ref.shape[1] // TILE, count // (TILE * GROUP)
    down = min(STEP_TILES // (GROUP * across), groups)
    slot_ref[0] = 0
    slot = slot_ref[0]
    if both:
        vc_ref[...] = halves(x_ref[DIMS:, :], BF16)
        facc_ref[...] = jnp.zeros_like(facc_ref)
    vr_ref[...] = halves(v_ref[DIMS:, start : start + count], BF16)
    acc_ref[...] = jnp.zeros_like(acc_ref)

    def distances(ref, i, j):
        rows = pl.ds(pl.multiple_of(start + i * TILE * GROUP, TILE * GROUP), TILE * GROUP)
        d2 = dot(at_ref[rows, :], b_ref[:, j * TILE : (j + 1) * TILE], 1, 0)
        ref[0] = jnp.maximum(d2, 1e-30)

    def products(hi, lo, i, j):
        cols = slice(j * TILE, (j + 1) * TILE)
        rows = pl.ds(pl.multiple_of(i * TILE, TILE), TILE)
        vr = vr_ref[:, rows]
        acc_ref[:, cols] += dot(vr, hi, 1, 0) + dot(vr, lo, 1, 0)
        if both:
            vc = vc_ref[:, cols]
            facc_ref[:, rows] += dot(vc, hi, 1, 1) + dot(vc, lo, 1, 1)

    hi_ref[...] = jnp.zeros_like(hi_ref)
    lo_ref[...] = jnp.zeros_like(lo_ref)
    distances(even_ref, 0, 0)

    def step(k, carry):
        hi, lo = hi_ref[...], lo_ref[...]
        i, j = jnp.maximum(k * down * GROUP - 1, 0), across - 1
        for t in range(down * across):
            now, later = (even_ref, odd_ref) if t % 2 == 0 else (odd_ref, even_ref)
            ahead = k * down + (t + 1) // across
            if t == down * across - 1:
                ahead = jnp.where(ahead < groups, ahead, 0)
            distances(later, ahead, (t + 1) % across)
            for g in range(GROUP):
                products(hi, lo, i, j)
                hi, lo = kernel_tile(now[slot, g * TILE : (g + 1) * TILE, :])
                i, j = (k * down + t // across) * GROUP + g, t % across
        hi_ref[...], lo_ref[...] = hi, lo
        return carry

    lax.fori_loop(0, groups // down, step, 0)
    products(hi_ref[...], lo_ref[...], groups * GROUP - 1, across - 1)
    bwd_ref[...] = fold(acc_ref[...])
    if both:
        fwd_ref[...] = fold(facc_ref[...])


VMEM = pl.BlockSpec(memory_space=pltpu.VMEM)
PARAMS = pltpu.CompilerParams(vmem_limit_bytes=40 * 2**20)


def first(x):
    n = x.shape[1]
    return pl.pallas_call(
        first_kernel,
        out_shape=(jax.ShapeDtypeStruct((n, DEPTH), BF16), jax.ShapeDtypeStruct((DEPTH, n), BF16)),
        in_specs=[VMEM],
        out_specs=(VMEM, VMEM),
        compiler_params=PARAMS,
        cost_estimate=pl.CostEstimate(flops=n * 64, bytes_accessed=n * 16, transcendentals=0),
        name="first",
    )(x)


def prep(x, rows):
    n = x.shape[1]
    return pl.pallas_call(
        rows_kernel if rows else cols_kernel,
        out_shape=jax.ShapeDtypeStruct((n, DEPTH) if rows else (DEPTH, n), BF16),
        in_specs=[VMEM],
        out_specs=VMEM,
        compiler_params=PARAMS,
        cost_estimate=pl.CostEstimate(flops=n * 64, bytes_accessed=n * 16, transcendentals=0),
        name="rows" if rows else "cols",
    )(x)


def tiles(at, v, b, x=None, start=0, n=None):
    n, width = n or at.shape[0], b.shape[1]
    both = x is not None
    bwd = jax.ShapeDtypeStruct((RHS, width), F32)
    fwd = jax.ShapeDtypeStruct((RHS, n), F32)
    more = [pltpu.VMEM((2 * RHS, width), BF16), pltpu.VMEM((2 * RHS, n), F32)] if both else []
    return pl.pallas_call(
        functools.partial(tile_kernel, both, start, n),
        out_shape=(fwd, bwd) if both else bwd,
        in_specs=[VMEM] * (4 if both else 3),
        out_specs=(VMEM, VMEM) if both else VMEM,
        scratch_shapes=more
        + [
            pltpu.VMEM((2 * RHS, n), BF16),
            pltpu.VMEM((2 * RHS, width), F32),
            pltpu.VMEM((1, TILE * GROUP, TILE), F32),
            pltpu.VMEM((1, TILE * GROUP, TILE), F32),
            pltpu.VMEM((TILE, TILE), BF16),
            pltpu.VMEM((TILE, TILE), LOW),
            pltpu.SMEM((1,), jnp.int32),
        ],
        compiler_params=PARAMS,
        cost_estimate=pl.CostEstimate(
            flops=n * width * 8, bytes_accessed=n * 16, transcendentals=0
        ),
        name="both" if both else "own",
    )(at, v, b, *([x] if both else []))


def shifted(value, steps):
    count = lax.axis_size("blk")
    return lax.ppermute(value, "blk", [(s, (s + steps) % count) for s in range(count)])


def swapped(value, mask):
    count = lax.axis_size("split")
    return lax.ppermute(value, "split", [(s, s ^ mask) for s in range(count)])


def after(value, *others):
    return lax.optimization_barrier((value, *others))[0]


def body(points, vectors, inv_length, noise):
    scaled = points * inv_length[:, None] * POINT_SCALE
    row = lax.broadcasted_iota(jnp.int32, (DIMS + RHS, points.shape[1]), 0)
    own = jnp.where(
        row < DIMS, jnp.pad(scaled, ((0, RHS), (0, 0))), jnp.pad(vectors, ((DIMS, 0), (0, 0)))
    )
    width = own.shape[1]
    near = swapped(own, 1)
    far = swapped(own, 2)
    two = shifted(own, 2)
    at0, b0 = first(own)
    total = tiles(at0, own, b0)
    near = after(near, total)
    at_near = prep(near, True)
    total = total + tiles(at_near, near, b0)
    far = after(far, total)
    cross = swapped(far, 1)
    one = shifted(after(own, far), 1)
    at_far = prep(far, True)
    b2 = prep(after(two, total), False)
    cross = after(cross, b2)
    at_cross = prep(cross, True)
    block = jnp.concatenate([own, far, cross, near], axis=1)
    at = jnp.concatenate([at0, at_far, at_cross, at_near], axis=0)
    fwd2, ret2 = tiles(at, block, b2, two)
    back2 = shifted(ret2, -2)
    one = after(one, ret2)
    b1 = prep(one, False)
    fwd_other, ret_other = tiles(at, block, b1, one, 2 * width, 2 * width)
    give_near = swapped(fwd_other + fwd2[:, 2 * width :], 1)
    fwd_pair, ret_pair = tiles(at, after(block, ret_other), b1, one, 0, 2 * width)
    back1 = shifted(ret_other + ret_pair, -1)
    rows = fwd_pair + fwd2[:, : 2 * width]
    rows_far = rows[:, width:] + give_near[:, :width]
    give_far = swapped(rows_far, 2)
    total = total + tiles(at, after(block, rows_far), b0, None, width, 2 * width)
    total = total + rows[:, :width] + give_near[:, width:]
    return total + give_far + back1 + back2 + noise[None, :] * vectors


def solution(mesh):
    placed = (P(None, ("blk", "split")), P(None, ("blk", "split")), P(), P(("blk", "split")))
    return jax.shard_map(
        body, mesh=mesh, in_specs=placed, out_specs=P(None, ("blk", "split")), check_vma=False
    )
```

```python
import functools

import jax
import jax.numpy as jnp
from jax import lax
from jax.experimental import pallas as pl
from jax.experimental.pallas import tpu as pltpu
from jax.sharding import PartitionSpec as P

SIGNAL = 0.03125
ROOT_FIVE = 2.23606797749979
LOG2E = 1.4426950408889634
POINT_SCALE = ROOT_FIVE * LOG2E
OUT_SCALE = SIGNAL / (3.0 * LOG2E * LOG2E)
SHIFT = 1.5 * LOG2E
FLOOR = 0.75 * LOG2E * LOG2E
LIFT = 14.0
DIMS = 32
RHS = 16
DEPTH = 256
TILE = 256
GROUP = 2
STEP_TILES = 32
BF16 = jnp.bfloat16
F32 = jnp.float32
F8 = jnp.float8_e4m3fn
PEAK = 128.0


def dot(a, b, ca, cb):
    return lax.dot_general(a, b, (((ca,), (cb,)), ((), ())), preferred_element_type=F32)


def pieces(x):
    hi = x.astype(BF16)
    rest = x - hi.astype(F32)
    mid = rest.astype(BF16)
    lo = (rest - mid.astype(F32)).astype(BF16)
    return hi, mid, lo


def norm_rows(sq, first):
    s1, s2, s3 = (p.astype(F32) for p in pieces(sq))
    row = lax.broadcasted_iota(jnp.int32, (16, sq.shape[1]), 0)
    out = jnp.where(row < 6, 1.0, 0.0)
    for k, s in enumerate((s1, s2, s3)):
        out = jnp.where(row == first + k, s, out)
    return out.astype(BF16)


def features(x, rows):
    sq = jnp.sum(x * x, axis=0, keepdims=True)
    hi, mid, lo = pieces(x)
    pad = jnp.zeros((DEPTH - 208, x.shape[1]), BF16)
    if rows:
        two = jnp.asarray(-2.0, BF16)
        hi, mid, lo = hi * two, mid * two, lo * two
        return jnp.concatenate([hi, mid, hi, lo, mid, hi, norm_rows(sq, 0), pad], axis=0)
    return jnp.concatenate([hi, hi, mid, hi, mid, lo, norm_rows(sq, 3), pad], axis=0)


def halves(v, kind):
    hi = v.astype(kind)
    return jnp.concatenate([hi, (v - hi.astype(F32)).astype(kind)], axis=0)


def kernel_tile(b2, low):
    if low == BF16:
        w = -SHIFT - b2 * lax.rsqrt(b2)
        t = (w * w + FLOOR) * jnp.exp2(w)
    else:
        b = b2 * lax.rsqrt(b2)
        t = ((b + 3.0 * LOG2E) * b + 3.0 * LOG2E * LOG2E) * jnp.exp2(LIFT - b)
    hi = t.astype(BF16)
    return hi, (t - hi.astype(F32)).astype(low)


def leveled(v, low):
    if low == BF16:
        return v, OUT_SCALE * 2.0**SHIFT
    top = jnp.maximum(jnp.max(jnp.abs(v), axis=1, keepdims=True), 1e-30)
    return v * (PEAK / top), top * (OUT_SCALE * 2.0**-LIFT / PEAK)


def fold(x, undo):
    return (x[:RHS] + x[RHS:]) * undo


def scaled(x_ref, inv):
    return (x_ref[:DIMS, :] * inv) * POINT_SCALE


def first_kernel(x_ref, inv_ref, at_ref, b_ref, inv_col_ref):
    row = lax.broadcasted_iota(jnp.int32, (DIMS, DIMS), 0)
    col = lax.broadcasted_iota(jnp.int32, (DIMS, DIMS), 1)
    inv = jnp.sum(jnp.where(row == col, inv_ref[...], 0.0), axis=1, keepdims=True)
    inv_col_ref[...] = jnp.broadcast_to(inv, inv_col_ref.shape)
    x = scaled(x_ref, inv)
    at_ref[...] = features(x, True).T
    b_ref[...] = features(x, False)


def rows_kernel(x_ref, inv_ref, at_ref):
    at_ref[...] = features(scaled(x_ref, inv_ref[:, :1]), True).T


def cols_kernel(x_ref, inv_ref, b_ref):
    b_ref[...] = features(scaled(x_ref, inv_ref[:, :1]), False)


def tile_kernel(both, low, start, count, at_ref, v_ref, b_ref, *rest):
    if both:
        x_ref, fwd_ref, bwd_ref, vc_ref, vc_low_ref, facc_ref = rest[:6]
    else:
        bwd_ref = rest[0]
    vr_ref, vr_low_ref, acc_ref, even_ref, odd_ref, hi_ref, lo_ref, slot_ref = rest[6 if both else 1 :]
    across, groups = b_ref.shape[1] // TILE, count // (TILE * GROUP)
    down = min(STEP_TILES // (GROUP * across), groups)
    slot_ref[0] = 0
    slot = slot_ref[0]
    if both:
        vc, undo_c = leveled(x_ref[DIMS:, :], low)
        vc_ref[...] = halves(vc, BF16)
        vc_low_ref[...] = halves(vc, low)
        facc_ref[...] = jnp.zeros_like(facc_ref)
    vr, undo_r = leveled(v_ref[DIMS:, start : start + count], low)
    vr_ref[...] = halves(vr, BF16)
    vr_low_ref[...] = halves(vr, low)
    acc_ref[...] = jnp.zeros_like(acc_ref)

    def distances(ref, i, j):
        rows = pl.ds(pl.multiple_of(start + i * TILE * GROUP, TILE * GROUP), TILE * GROUP)
        d2 = dot(at_ref[rows, :], b_ref[:, j * TILE : (j + 1) * TILE], 1, 0)
        ref[0] = jnp.maximum(d2, 1e-30)

    def products(hi, lo, i, j):
        cols = slice(j * TILE, (j + 1) * TILE)
        rows = pl.ds(pl.multiple_of(i * TILE, TILE), TILE)
        acc_ref[:, cols] += dot(vr_ref[:, rows], hi, 1, 0) + dot(vr_low_ref[:, rows], lo, 1, 0)
        if both:
            facc_ref[:, rows] += dot(vc_ref[:, cols], hi, 1, 1) + dot(vc_low_ref[:, cols], lo, 1, 1)

    hi_ref[...] = jnp.zeros_like(hi_ref)
    lo_ref[...] = jnp.zeros_like(lo_ref)
    distances(even_ref, 0, 0)

    def step(k, carry):
        hi, lo = hi_ref[...], lo_ref[...]
        i, j = jnp.maximum(k * down * GROUP - 1, 0), across - 1
        for t in range(down * across):
            now, later = (even_ref, odd_ref) if t % 2 == 0 else (odd_ref, even_ref)
            ahead = k * down + (t + 1) // across
            if t == down * across - 1:
                ahead = jnp.where(ahead < groups, ahead, 0)
            distances(later, ahead, (t + 1) % across)
            for g in range(GROUP):
                products(hi, lo, i, j)
                hi, lo = kernel_tile(now[slot, g * TILE : (g + 1) * TILE, :], low)
                i, j = (k * down + t // across) * GROUP + g, t % across
        hi_ref[...], lo_ref[...] = hi, lo
        return carry

    lax.fori_loop(0, groups // down, step, 0)
    products(hi_ref[...], lo_ref[...], groups * GROUP - 1, across - 1)
    bwd_ref[...] = fold(acc_ref[...], undo_r)
    if both:
        fwd_ref[...] = fold(facc_ref[...], undo_c)


VMEM = pl.BlockSpec(memory_space=pltpu.VMEM)
PARAMS = pltpu.CompilerParams(vmem_limit_bytes=40 * 2**20)


def first(x, inv):
    n = x.shape[1]
    return pl.pallas_call(
        first_kernel,
        out_shape=(
            jax.ShapeDtypeStruct((n, DEPTH), BF16),
            jax.ShapeDtypeStruct((DEPTH, n), BF16),
            jax.ShapeDtypeStruct((DIMS, 128), F32),
        ),
        in_specs=[VMEM, VMEM],
        out_specs=(VMEM, VMEM, VMEM),
        compiler_params=PARAMS,
        cost_estimate=pl.CostEstimate(flops=n * 64, bytes_accessed=n * 16, transcendentals=0),
        name="first",
    )(x, inv)


def prep(x, inv, rows):
    n = x.shape[1]
    return pl.pallas_call(
        rows_kernel if rows else cols_kernel,
        out_shape=jax.ShapeDtypeStruct((n, DEPTH) if rows else (DEPTH, n), BF16),
        in_specs=[VMEM, VMEM],
        out_specs=VMEM,
        compiler_params=PARAMS,
        cost_estimate=pl.CostEstimate(flops=n * 64, bytes_accessed=n * 16, transcendentals=0),
        name="rows" if rows else "cols",
    )(x, inv)


def tiles(at, v, b, x=None, start=0, n=None):
    n, width = n or at.shape[0], b.shape[1]
    both = x is not None
    low = F8 if both else BF16
    bwd = jax.ShapeDtypeStruct((RHS, width), F32)
    fwd = jax.ShapeDtypeStruct((RHS, n), F32)
    more = [
        pltpu.VMEM((2 * RHS, width), BF16),
        pltpu.VMEM((2 * RHS, width), low),
        pltpu.VMEM((2 * RHS, n), F32),
    ]
    return pl.pallas_call(
        functools.partial(tile_kernel, both, low, start, n),
        out_shape=(fwd, bwd) if both else bwd,
        in_specs=[VMEM] * (4 if both else 3),
        out_specs=(VMEM, VMEM) if both else VMEM,
        scratch_shapes=(more if both else [])
        + [
            pltpu.VMEM((2 * RHS, n), BF16),
            pltpu.VMEM((2 * RHS, n), low),
            pltpu.VMEM((2 * RHS, width), F32),
            pltpu.VMEM((1, TILE * GROUP, TILE), F32),
            pltpu.VMEM((1, TILE * GROUP, TILE), F32),
            pltpu.VMEM((TILE, TILE), BF16),
            pltpu.VMEM((TILE, TILE), low),
            pltpu.SMEM((1,), jnp.int32),
        ],
        compiler_params=PARAMS,
        cost_estimate=pl.CostEstimate(
            flops=n * width * 8, bytes_accessed=n * 16, transcendentals=0
        ),
        name="both" if both else "own",
    )(at, v, b, *([x] if both else []))


def shifted(value, steps):
    count = lax.axis_size("blk")
    return lax.ppermute(value, "blk", [(s, (s + steps) % count) for s in range(count)])


def swapped(value, mask):
    count = lax.axis_size("split")
    return lax.ppermute(value, "split", [(s, s ^ mask) for s in range(count)])


def after(value, *others):
    return lax.optimization_barrier((value, *others))[0]


def body(points, vectors, inv_length, noise):
    row = lax.broadcasted_iota(jnp.int32, (DIMS + RHS, points.shape[1]), 0)
    own = jnp.where(row < DIMS, jnp.pad(points, ((0, RHS), (0, 0))), jnp.pad(vectors, ((DIMS, 0), (0, 0))))
    width = own.shape[1]
    near = swapped(own, 1)
    far = swapped(own, 2)
    two = shifted(own, 2)
    at0, b0, inv = first(own, inv_length.reshape(1, DIMS))
    total = tiles(at0, own, b0)
    near = after(near, total)
    at_near = prep(near, inv, True)
    total = total + tiles(at_near, near, b0)
    far = after(far, total)
    cross = swapped(far, 1)
    one = shifted(after(own, far), 1)
    at_far = prep(far, inv, True)
    b2 = prep(after(two, total), inv, False)
    cross = after(cross, b2)
    at_cross = prep(cross, inv, True)
    block = jnp.concatenate([own, far, cross, near], axis=1)
    at = jnp.concatenate([at0, at_far, at_cross, at_near], axis=0)
    fwd2, ret2 = tiles(at, block, b2, two)
    back2 = shifted(ret2, -2)
    one = after(one, ret2)
    b1 = prep(one, inv, False)
    fwd_other, ret_other = tiles(at, block, b1, one, 2 * width, 2 * width)
    give_near = swapped(fwd_other + fwd2[:, 2 * width :], 1)
    fwd_pair, ret_pair = tiles(at, after(block, ret_other), b1, one, 0, 2 * width)
    back1 = shifted(ret_other + ret_pair, -1)
    rows = fwd_pair + fwd2[:, : 2 * width]
    rows_far = rows[:, width:] + give_near[:, :width]
    give_far = swapped(rows_far, 2)
    total = total + tiles(at, after(block, rows_far), b0, None, width, 2 * width)
    total = total + rows[:, :width] + give_near[:, width:]
    return total + give_far + back1 + back2 + noise[None, :] * vectors


def solution(mesh):
    placed = (P(None, ("blk", "split")), P(None, ("blk", "split")), P(), P(("blk", "split")))
    return jax.shard_map(
        body, mesh=mesh, in_specs=placed, out_specs=P(None, ("blk", "split")), check_vma=False
    )
```

```python
import functools

import jax
import jax.numpy as jnp
from jax import lax
from jax.experimental import pallas as pl
from jax.experimental.pallas import tpu as pltpu
from jax.sharding import PartitionSpec as P

SIGNAL = 0.03125
ROOT_FIVE = 2.23606797749979
LOG2E = 1.4426950408889634
POINT_SCALE = ROOT_FIVE * LOG2E
OUT_SCALE = SIGNAL / (3.0 * LOG2E * LOG2E)
SHIFT = 1.5 * LOG2E
FLOOR = 0.75 * LOG2E * LOG2E
LIFT = 14.0
DIMS = 32
RHS = 16
DEPTH = 256
TILE = 256
GROUP = 2
BF16 = jnp.bfloat16
F32 = jnp.float32
F8 = jnp.float8_e4m3fn
PEAK = 128.0


def dot(a, b, ca, cb):
    return lax.dot_general(a, b, (((ca,), (cb,)), ((), ())), preferred_element_type=F32)


def pieces(x):
    hi = x.astype(BF16)
    rest = x - hi.astype(F32)
    mid = rest.astype(BF16)
    lo = (rest - mid.astype(F32)).astype(BF16)
    return hi, mid, lo


def norm_rows(sq, first):
    s1, s2, s3 = (p.astype(F32) for p in pieces(sq))
    row = lax.broadcasted_iota(jnp.int32, (16, sq.shape[1]), 0)
    out = jnp.where(row < 6, 1.0, 0.0)
    for k, s in enumerate((s1, s2, s3)):
        out = jnp.where(row == first + k, s, out)
    return out.astype(BF16)


def features(x, rows):
    sq = jnp.sum(x * x, axis=0, keepdims=True)
    hi, mid, lo = pieces(x)
    pad = jnp.zeros((DEPTH - 208, x.shape[1]), BF16)
    if rows:
        two = jnp.asarray(-2.0, BF16)
        hi, mid, lo = hi * two, mid * two, lo * two
        return jnp.concatenate([hi, mid, hi, lo, mid, hi, norm_rows(sq, 0), pad], axis=0)
    return jnp.concatenate([hi, hi, mid, hi, mid, lo, norm_rows(sq, 3), pad], axis=0)


def halves(v, kind):
    hi = v.astype(kind)
    return jnp.concatenate([hi, (v - hi.astype(F32)).astype(kind)], axis=0)


def kernel_tile(b2, low):
    if low == BF16:
        w = -SHIFT - b2 * lax.rsqrt(b2)
        t = (w * w + FLOOR) * jnp.exp2(w)
    else:
        b = b2 * lax.rsqrt(b2)
        t = ((b + 3.0 * LOG2E) * b + 3.0 * LOG2E * LOG2E) * jnp.exp2(LIFT - b)
    hi = t.astype(BF16)
    return hi, (t - hi.astype(F32)).astype(low)


def leveled(v, low):
    if low == BF16:
        return v, OUT_SCALE * 2.0**SHIFT
    top = jnp.maximum(jnp.max(jnp.abs(v), axis=1, keepdims=True), 1e-30)
    return v * (PEAK / top), top * (OUT_SCALE * 2.0**-LIFT / PEAK)


def fold(x, undo):
    return (x[:RHS] + x[RHS:]) * undo


def scaled(x_ref, inv):
    return (x_ref[:DIMS, :] * inv) * POINT_SCALE


def first_kernel(x_ref, inv_ref, at_ref, b_ref, inv_col_ref):
    row = lax.broadcasted_iota(jnp.int32, (DIMS, DIMS), 0)
    col = lax.broadcasted_iota(jnp.int32, (DIMS, DIMS), 1)
    inv = jnp.sum(jnp.where(row == col, inv_ref[...], 0.0), axis=1, keepdims=True)
    inv_col_ref[...] = jnp.broadcast_to(inv, inv_col_ref.shape)
    x = scaled(x_ref, inv)
    at_ref[...] = features(x, True).T
    b_ref[...] = features(x, False)


def rows_kernel(x_ref, inv_ref, at_ref):
    at_ref[...] = features(scaled(x_ref, inv_ref[:, :1]), True).T


def cols_kernel(x_ref, inv_ref, b_ref):
    b_ref[...] = features(scaled(x_ref, inv_ref[:, :1]), False)


def tile_kernel(both, low, count, *refs):
    ats, vs, b_ref, rest = refs[:count], refs[count : 2 * count], refs[2 * count], refs[2 * count + 1 :]
    if both:
        x_ref, fwd_ref, bwd_ref, vc_ref, vc_low_ref, facc_ref = rest[:6]
    else:
        bwd_ref = rest[0]
    vr_ref, vr_low_ref, acc_ref, even_ref, odd_ref, slot_ref = rest[6 if both else 1 :]
    part = ats[0].shape[0]
    across, per_part = b_ref.shape[1] // TILE, part // (TILE * GROUP)
    slot_ref[0] = 0
    slot = slot_ref[0]
    if both:
        vc, undo_c = leveled(x_ref[DIMS:, :], low)
        vc_ref[...] = halves(vc, BF16)
        vc_low_ref[...] = halves(vc, low)
        facc_ref[...] = jnp.zeros_like(facc_ref)
    vr, undo_r = leveled(jnp.concatenate([v[DIMS:, :] for v in vs], axis=1), low)
    vr_ref[...] = halves(vr, BF16)
    vr_low_ref[...] = halves(vr, low)
    acc_ref[...] = jnp.zeros_like(acc_ref)

    def distances(ref, group, j):
        first = group % per_part * TILE * GROUP
        rows = ats[group // per_part][first : first + TILE * GROUP, :]
        ref[0] = jnp.maximum(dot(rows, b_ref[:, j * TILE : (j + 1) * TILE], 1, 0), 1e-30)

    def products(hi, lo, i, j):
        rows, cols = slice(i * TILE, (i + 1) * TILE), slice(j * TILE, (j + 1) * TILE)
        acc_ref[:, cols] += dot(vr_ref[:, rows], hi, 1, 0) + dot(vr_low_ref[:, rows], lo, 1, 0)
        if both:
            facc_ref[:, rows] += dot(vc_ref[:, cols], hi, 1, 1) + dot(vc_low_ref[:, cols], lo, 1, 1)

    behind = None
    groups = [(i, j) for i in range(count * per_part) for j in range(across)]
    distances(even_ref, 0, 0)
    for t, (i, j) in enumerate(groups):
        now, later = (even_ref, odd_ref) if t % 2 == 0 else (odd_ref, even_ref)
        if t + 1 < len(groups):
            distances(later, *groups[t + 1])
        for g in range(GROUP):
            if behind is not None:
                products(*behind)
            hi, lo = kernel_tile(now[slot, g * TILE : (g + 1) * TILE, :], low)
            behind = hi, lo, i * GROUP + g, j
    products(*behind)
    bwd_ref[...] = fold(acc_ref[...], undo_r)
    if both:
        fwd_ref[...] = fold(facc_ref[...], undo_c)


VMEM = pl.BlockSpec(memory_space=pltpu.VMEM)
PARAMS = pltpu.CompilerParams(vmem_limit_bytes=40 * 2**20)


def first(x, inv):
    n = x.shape[1]
    return pl.pallas_call(
        first_kernel,
        out_shape=(
            jax.ShapeDtypeStruct((n, DEPTH), BF16),
            jax.ShapeDtypeStruct((DEPTH, n), BF16),
            jax.ShapeDtypeStruct((DIMS, 128), F32),
        ),
        in_specs=[VMEM, VMEM],
        out_specs=(VMEM, VMEM, VMEM),
        compiler_params=PARAMS,
        cost_estimate=pl.CostEstimate(flops=n * 64, bytes_accessed=n * 16, transcendentals=0),
        name="first",
    )(x, inv)


def prep(x, inv, rows):
    n = x.shape[1]
    return pl.pallas_call(
        rows_kernel if rows else cols_kernel,
        out_shape=jax.ShapeDtypeStruct((n, DEPTH) if rows else (DEPTH, n), BF16),
        in_specs=[VMEM, VMEM],
        out_specs=VMEM,
        compiler_params=PARAMS,
        cost_estimate=pl.CostEstimate(flops=n * 64, bytes_accessed=n * 16, transcendentals=0),
        name="rows" if rows else "cols",
    )(x, inv)


def tiles(ats, vs, b, x=None):
    n, width = len(ats) * ats[0].shape[0], b.shape[1]
    both = x is not None
    low = F8 if both else BF16
    bwd = jax.ShapeDtypeStruct((RHS, width), F32)
    fwd = jax.ShapeDtypeStruct((RHS, n), F32)
    more = [
        pltpu.VMEM((2 * RHS, width), BF16),
        pltpu.VMEM((2 * RHS, width), low),
        pltpu.VMEM((2 * RHS, n), F32),
    ]
    return pl.pallas_call(
        functools.partial(tile_kernel, both, low, len(ats)),
        out_shape=(fwd, bwd) if both else bwd,
        in_specs=[VMEM] * (2 * len(ats) + (2 if both else 1)),
        out_specs=(VMEM, VMEM) if both else VMEM,
        scratch_shapes=(more if both else [])
        + [
            pltpu.VMEM((2 * RHS, n), BF16),
            pltpu.VMEM((2 * RHS, n), low),
            pltpu.VMEM((2 * RHS, width), F32),
            pltpu.VMEM((1, TILE * GROUP, TILE), F32),
            pltpu.VMEM((1, TILE * GROUP, TILE), F32),
            pltpu.SMEM((1,), jnp.int32),
        ],
        compiler_params=PARAMS,
        cost_estimate=pl.CostEstimate(
            flops=n * width * 8, bytes_accessed=n * 16, transcendentals=0
        ),
        name="both" if both else "own",
    )(*ats, *vs, b, *([x] if both else []))


def shifted(value, steps):
    count = lax.axis_size("blk")
    return lax.ppermute(value, "blk", [(s, (s + steps) % count) for s in range(count)])


def swapped(value, mask):
    count = lax.axis_size("split")
    return lax.ppermute(value, "split", [(s, s ^ mask) for s in range(count)])


def after(value, *others):
    return lax.optimization_barrier((value, *others))[0]


def body(points, vectors, inv_length, noise):
    row = lax.broadcasted_iota(jnp.int32, (DIMS + RHS, points.shape[1]), 0)
    own = jnp.where(row < DIMS, jnp.pad(points, ((0, RHS), (0, 0))), jnp.pad(vectors, ((DIMS, 0), (0, 0))))
    width = own.shape[1]
    near = swapped(own, 1)
    far = swapped(own, 2)
    two = shifted(own, 2)
    at0, b0, inv = first(own, inv_length.reshape(1, DIMS))
    total = tiles([at0], [own], b0)
    near = after(near, total)
    at_near = prep(near, inv, True)
    total = total + tiles([at_near], [near], b0)
    far = after(far, total)
    cross = swapped(far, 1)
    one = shifted(after(own, far), 1)
    at_far = prep(far, inv, True)
    b2 = prep(after(two, total), inv, False)
    cross = after(cross, b2)
    at_cross = prep(cross, inv, True)
    fwd2, ret2 = tiles([at0, at_far, at_cross, at_near], [own, far, cross, near], b2, two)
    back2 = shifted(ret2, -2)
    one = after(one, ret2)
    b1 = prep(one, inv, False)
    fwd_other, ret_other = tiles([at_cross, at_near], [cross, near], b1, one)
    give_near = swapped(fwd_other + fwd2[:, 2 * width :], 1)
    fwd_pair, ret_pair = tiles([at0, after(at_far, ret_other)], [own, far], b1, one)
    back1 = shifted(ret_other + ret_pair, -1)
    rows = fwd_pair + fwd2[:, : 2 * width]
    rows_far = rows[:, width:] + give_near[:, :width]
    give_far = swapped(rows_far, 2)
    total = total + tiles([at_far, after(at_cross, rows_far)], [far, cross], b0)
    total = total + rows[:, :width] + give_near[:, width:]
    return total + give_far + back1 + back2 + noise[None, :] * vectors


def solution(mesh):
    placed = (P(None, ("blk", "split")), P(None, ("blk", "split")), P(), P(("blk", "split")))
    return jax.shard_map(
        body, mesh=mesh, in_specs=placed, out_specs=P(None, ("blk", "split")), check_vma=False
    )
```

```python
import functools

import jax
import jax.numpy as jnp
from jax import lax
from jax.experimental import pallas as pl
from jax.experimental.pallas import tpu as pltpu
from jax.sharding import PartitionSpec as P

SIGNAL = 0.03125
ROOT_FIVE = 2.23606797749979
LOG2E = 1.4426950408889634
POINT_SCALE = ROOT_FIVE * LOG2E
OUT_SCALE = SIGNAL / (3.0 * LOG2E * LOG2E)
SHIFT = 1.5 * LOG2E
FLOOR = 0.75 * LOG2E * LOG2E
LIFT = 14.0
DIMS = 32
RHS = 16
DEPTH = 256
TILE = 256
GROUP = 2
BF16 = jnp.bfloat16
F32 = jnp.float32
F8 = jnp.float8_e4m3fn
PEAK = 128.0


def dot(a, b, ca, cb):
    return lax.dot_general(a, b, (((ca,), (cb,)), ((), ())), preferred_element_type=F32)


def pieces(x):
    hi = x.astype(BF16)
    rest = x - hi.astype(F32)
    mid = rest.astype(BF16)
    lo = (rest - mid.astype(F32)).astype(BF16)
    return hi, mid, lo


def norm_rows(sq, first):
    s1, s2, s3 = (p.astype(F32) for p in pieces(sq))
    row = lax.broadcasted_iota(jnp.int32, (16, sq.shape[1]), 0)
    out = jnp.where(row < 6, 1.0, 0.0)
    for k, s in enumerate((s1, s2, s3)):
        out = jnp.where(row == first + k, s, out)
    return out.astype(BF16)


def features(x, rows):
    sq = jnp.sum(x * x, axis=0, keepdims=True)
    hi, mid, lo = pieces(x)
    pad = jnp.zeros((DEPTH - 208, x.shape[1]), BF16)
    if rows:
        two = jnp.asarray(-2.0, BF16)
        hi, mid, lo = hi * two, mid * two, lo * two
        return jnp.concatenate([hi, mid, hi, lo, mid, hi, norm_rows(sq, 0), pad], axis=0)
    return jnp.concatenate([hi, hi, mid, hi, mid, lo, norm_rows(sq, 3), pad], axis=0)


def halves(v, kind):
    hi = v.astype(kind)
    return jnp.concatenate([hi, (v - hi.astype(F32)).astype(kind)], axis=0)


def kernel_tile(b2, low):
    if low == BF16:
        w = -SHIFT - b2 * lax.rsqrt(b2)
        t = (w * w + FLOOR) * jnp.exp2(w)
    else:
        b = b2 * lax.rsqrt(b2)
        t = ((b + 3.0 * LOG2E) * b + 3.0 * LOG2E * LOG2E) * jnp.exp2(LIFT - b)
    hi = t.astype(BF16)
    return hi, (t - hi.astype(F32)).astype(low)


def leveled(v, low):
    if low == BF16:
        return v, OUT_SCALE * 2.0**SHIFT
    top = jnp.maximum(jnp.max(jnp.abs(v), axis=1, keepdims=True), 1e-30)
    return v * (PEAK / top), top * (OUT_SCALE * 2.0**-LIFT / PEAK)


def fold(x, undo):
    return (x[:RHS] + x[RHS:]) * undo


def scaled(x_ref, inv):
    return (x_ref[:DIMS, :] * inv) * POINT_SCALE


def first_kernel(x_ref, inv_ref, at_ref, b_ref, inv_col_ref):
    row = lax.broadcasted_iota(jnp.int32, (DIMS, DIMS), 0)
    col = lax.broadcasted_iota(jnp.int32, (DIMS, DIMS), 1)
    inv = jnp.sum(jnp.where(row == col, inv_ref[...], 0.0), axis=1, keepdims=True)
    inv_col_ref[...] = jnp.broadcast_to(inv, inv_col_ref.shape)
    x = scaled(x_ref, inv)
    at_ref[...] = features(x, True).T
    b_ref[...] = features(x, False)


def rows_kernel(x_ref, inv_ref, at_ref):
    at_ref[...] = features(scaled(x_ref, inv_ref[:, :1]), True).T


def cols_kernel(x_ref, inv_ref, b_ref):
    b_ref[...] = features(scaled(x_ref, inv_ref[:, :1]), False)


def tile_kernel(both, low, count, *refs):
    ats, vs, b_ref, rest = refs[:count], refs[count : 2 * count], refs[2 * count], refs[2 * count + 1 :]
    if both:
        x_ref, fwd_ref, bwd_ref, vc_ref, vc_low_ref, facc_ref = rest[:6]
    else:
        bwd_ref = rest[0]
    vr_ref, vr_low_ref, acc_ref, even_ref, odd_ref, slot_ref = rest[6 if both else 1 :]
    part = ats[0].shape[0]
    across, per_part = b_ref.shape[1] // TILE, part // (TILE * GROUP)
    slot_ref[0] = 0
    slot = slot_ref[0]
    if both:
        vc, undo_c = leveled(x_ref[DIMS:, :], low)
        vc_ref[...] = halves(vc, BF16)
        vc_low_ref[...] = halves(vc, low)
        facc_ref[...] = jnp.zeros_like(facc_ref)
    vr, undo_r = leveled(jnp.concatenate([v[DIMS:, :] for v in vs], axis=1), low)
    vr_ref[...] = halves(vr, BF16)
    vr_low_ref[...] = halves(vr, low)
    acc_ref[...] = jnp.zeros_like(acc_ref)

    def distances(ref, group, j):
        first = group % per_part * TILE * GROUP
        rows = ats[group // per_part][first : first + TILE * GROUP, :]
        ref[0] = jnp.maximum(dot(rows, b_ref[:, j * TILE : (j + 1) * TILE], 1, 0), 1e-30)

    def products(hi, lo, i, j):
        rows, cols = slice(i * TILE, (i + 1) * TILE), slice(j * TILE, (j + 1) * TILE)
        acc_ref[:, cols] += dot(vr_ref[:, rows], hi, 1, 0) + dot(vr_low_ref[:, rows], lo, 1, 0)
        if both:
            facc_ref[:, rows] += dot(vc_ref[:, cols], hi, 1, 1) + dot(vc_low_ref[:, cols], lo, 1, 1)

    behind = None
    groups = [(i, j) for i in range(count * per_part) for j in range(across)]
    distances(even_ref, 0, 0)
    for t, (i, j) in enumerate(groups):
        now, later = (even_ref, odd_ref) if t % 2 == 0 else (odd_ref, even_ref)
        if t + 1 < len(groups):
            distances(later, *groups[t + 1])
        for g in range(GROUP):
            if behind is not None:
                products(*behind)
            hi, lo = kernel_tile(now[slot, g * TILE : (g + 1) * TILE, :], low)
            behind = hi, lo, i * GROUP + g, j
    products(*behind)
    bwd_ref[...] = fold(acc_ref[...], undo_r)
    if both:
        fwd_ref[...] = fold(facc_ref[...], undo_c)


VMEM = pl.BlockSpec(memory_space=pltpu.VMEM)
PARAMS = pltpu.CompilerParams(vmem_limit_bytes=40 * 2**20)


def first(x, inv):
    n = x.shape[1]
    return pl.pallas_call(
        first_kernel,
        out_shape=(
            jax.ShapeDtypeStruct((n, DEPTH), BF16),
            jax.ShapeDtypeStruct((DEPTH, n), BF16),
            jax.ShapeDtypeStruct((DIMS, 128), F32),
        ),
        in_specs=[VMEM, VMEM],
        out_specs=(VMEM, VMEM, VMEM),
        compiler_params=PARAMS,
        cost_estimate=pl.CostEstimate(flops=n * 64, bytes_accessed=n * 16, transcendentals=0),
        name="first",
    )(x, inv)


def prep(x, inv, rows):
    n = x.shape[1]
    return pl.pallas_call(
        rows_kernel if rows else cols_kernel,
        out_shape=jax.ShapeDtypeStruct((n, DEPTH) if rows else (DEPTH, n), BF16),
        in_specs=[VMEM, VMEM],
        out_specs=VMEM,
        compiler_params=PARAMS,
        cost_estimate=pl.CostEstimate(flops=n * 64, bytes_accessed=n * 16, transcendentals=0),
        name="rows" if rows else "cols",
    )(x, inv)


def tiles(ats, vs, b, x=None):
    n, width = len(ats) * ats[0].shape[0], b.shape[1]
    both = x is not None
    low = F8 if both else BF16
    bwd = jax.ShapeDtypeStruct((RHS, width), F32)
    fwd = jax.ShapeDtypeStruct((RHS, n), F32)
    more = [
        pltpu.VMEM((2 * RHS, width), BF16),
        pltpu.VMEM((2 * RHS, width), low),
        pltpu.VMEM((2 * RHS, n), F32),
    ]
    return pl.pallas_call(
        functools.partial(tile_kernel, both, low, len(ats)),
        out_shape=(fwd, bwd) if both else bwd,
        in_specs=[VMEM] * (2 * len(ats) + (2 if both else 1)),
        out_specs=(VMEM, VMEM) if both else VMEM,
        scratch_shapes=(more if both else [])
        + [
            pltpu.VMEM((2 * RHS, n), BF16),
            pltpu.VMEM((2 * RHS, n), low),
            pltpu.VMEM((2 * RHS, width), F32),
            pltpu.VMEM((1, TILE * GROUP, TILE), F32),
            pltpu.VMEM((1, TILE * GROUP, TILE), F32),
            pltpu.SMEM((1,), jnp.int32),
        ],
        compiler_params=PARAMS,
        cost_estimate=pl.CostEstimate(
            flops=n * width * 8, bytes_accessed=n * 16, transcendentals=0
        ),
        name="both" if both else "own",
    )(*ats, *vs, b, *([x] if both else []))


def shifted(value, steps):
    count = lax.axis_size("blk")
    return lax.ppermute(value, "blk", [(s, (s + steps) % count) for s in range(count)])


def swapped(value, mask):
    count = lax.axis_size("split")
    return lax.ppermute(value, "split", [(s, s ^ mask) for s in range(count)])


def after(value, *others):
    return lax.optimization_barrier((value, *others))[0]


def body(points, vectors, inv_length, noise):
    row = lax.broadcasted_iota(jnp.int32, (DIMS + RHS, points.shape[1]), 0)
    own = jnp.where(row < DIMS, jnp.pad(points, ((0, RHS), (0, 0))), jnp.pad(vectors, ((DIMS, 0), (0, 0))))
    width = own.shape[1]
    near = swapped(own, 1)
    far = swapped(own, 2)
    two = shifted(own, 2)
    at0, b0, inv = first(own, inv_length.reshape(1, DIMS))
    total = tiles([at0], [own], b0)
    near = after(near, total)
    at_near = prep(near, inv, True)
    total = total + tiles([at_near], [near], b0)
    far = after(far, total)
    cross = swapped(far, 1)
    one = shifted(after(own, far), 1)
    at_far = prep(far, inv, True)
    b2 = prep(after(two, total), inv, False)
    cross = after(cross, b2)
    at_cross = prep(cross, inv, True)
    fwd2, ret2 = tiles([at0, at_far, at_cross, at_near], [own, far, cross, near], b2, two)
    back2 = shifted(ret2, -2)
    one = after(one, ret2)
    fwd1, ret1 = tiles([at0, at_far, at_cross, at_near], [own, far, cross, near], prep(one, inv, False), one)
    back1 = shifted(ret1, -1)
    fwd = fwd1 + fwd2
    give_near = swapped(fwd[:, 2 * width :], 1)
    rows_far = fwd[:, width : 2 * width] + give_near[:, :width]
    give_far = swapped(rows_far, 2)
    total = total + tiles([at_far, after(at_cross, rows_far)], [far, cross], b0)
    total = total + fwd[:, :width] + give_near[:, width:]
    return total + give_far + back1 + back2 + noise[None, :] * vectors


def solution(mesh):
    placed = (P(None, ("blk", "split")), P(None, ("blk", "split")), P(), P(("blk", "split")))
    return jax.shard_map(
        body, mesh=mesh, in_specs=placed, out_specs=P(None, ("blk", "split")), check_vma=False
    )
```

```python
import functools

import jax
import jax.numpy as jnp
from jax import lax
from jax.experimental import pallas as pl
from jax.experimental.pallas import tpu as pltpu
from jax.sharding import PartitionSpec as P

SIGNAL = 0.03125
ROOT_FIVE = 2.23606797749979
LOG2E = 1.4426950408889634
POINT_SCALE = ROOT_FIVE * LOG2E
OUT_SCALE = SIGNAL / (3.0 * LOG2E * LOG2E)
SHIFT = 1.5 * LOG2E
FLOOR = 0.75 * LOG2E * LOG2E
LIFT = 14.0
DIMS = 32
RHS = 16
DEPTH = 256
TILE = 256
GROUP = 2
BF16 = jnp.bfloat16
F32 = jnp.float32
F8 = jnp.float8_e4m3fn
PEAK = 128.0


def dot(a, b, ca, cb):
    return lax.dot_general(a, b, (((ca,), (cb,)), ((), ())), preferred_element_type=F32)


def pieces(x):
    hi = x.astype(BF16)
    rest = x - hi.astype(F32)
    mid = rest.astype(BF16)
    lo = (rest - mid.astype(F32)).astype(BF16)
    return hi, mid, lo


def norm_rows(sq, first):
    s1, s2, s3 = (p.astype(F32) for p in pieces(sq))
    row = lax.broadcasted_iota(jnp.int32, (16, sq.shape[1]), 0)
    out = jnp.where(row < 6, 1.0, 0.0)
    for k, s in enumerate((s1, s2, s3)):
        out = jnp.where(row == first + k, s, out)
    return out.astype(BF16)


def features(x, rows):
    sq = jnp.sum(x * x, axis=0, keepdims=True)
    hi, mid, lo = pieces(x)
    pad = jnp.zeros((DEPTH - 208, x.shape[1]), BF16)
    if rows:
        two = jnp.asarray(-2.0, BF16)
        hi, mid, lo = hi * two, mid * two, lo * two
        return jnp.concatenate([hi, mid, hi, lo, mid, hi, norm_rows(sq, 0), pad], axis=0)
    return jnp.concatenate([hi, hi, mid, hi, mid, lo, norm_rows(sq, 3), pad], axis=0)


def put_columns(b_ref, b):
    for k in range(b_ref.shape[0]):
        b_ref[k] = b[:, k * 128 : (k + 1) * 128]


def halves(v, kind):
    hi = v.astype(kind)
    return jnp.concatenate([hi, (v - hi.astype(F32)).astype(kind)], axis=0)


def kernel_tile(b2, low):
    if low == BF16:
        w = -SHIFT - b2 * lax.rsqrt(b2)
        t = (w * w + FLOOR) * jnp.exp2(w)
    else:
        b = b2 * lax.rsqrt(b2)
        t = ((b + 3.0 * LOG2E) * b + 3.0 * LOG2E * LOG2E) * jnp.exp2(LIFT - b)
    hi = t.astype(BF16)
    return hi, (t - hi.astype(F32)).astype(low)


def leveled(v, low):
    if low == BF16:
        return v, OUT_SCALE * 2.0**SHIFT
    top = jnp.maximum(jnp.max(jnp.abs(v), axis=1, keepdims=True), 1e-30)
    return v * (PEAK / top), top * (OUT_SCALE * 2.0**-LIFT / PEAK)


def fold(x, undo):
    return (x[:RHS] + x[RHS:]) * undo


def scaled(x_ref, inv):
    return (x_ref[:DIMS, :] * inv) * POINT_SCALE


def first_kernel(x_ref, inv_ref, at_ref, b_ref, inv_col_ref):
    row = lax.broadcasted_iota(jnp.int32, (DIMS, DIMS), 0)
    col = lax.broadcasted_iota(jnp.int32, (DIMS, DIMS), 1)
    inv = jnp.sum(jnp.where(row == col, inv_ref[...], 0.0), axis=1, keepdims=True)
    inv_col_ref[...] = jnp.broadcast_to(inv, inv_col_ref.shape)
    x = scaled(x_ref, inv)
    at_ref[...] = features(x, True).T
    put_columns(b_ref, features(x, False))


def rows_kernel(x_ref, inv_ref, at_ref):
    at_ref[...] = features(scaled(x_ref, inv_ref[:, :1]), True).T


def cols_kernel(x_ref, inv_ref, b_ref):
    put_columns(b_ref, features(scaled(x_ref, inv_ref[:, :1]), False))


def tile_kernel(both, low, count, *refs):
    ats, vs, b_ref, rest = refs[:count], refs[count : 2 * count], refs[2 * count], refs[2 * count + 1 :]
    if both:
        x_ref, fwd_ref, bwd_ref, vc_ref, vc_low_ref, facc_ref = rest[:6]
    else:
        bwd_ref = rest[0]
    vr_ref, vr_low_ref, acc_ref, even_ref, odd_ref, slot_ref = rest[6 if both else 1 :]
    part = ats[0].shape[0]
    across, per_part = b_ref.shape[0] * 128 // TILE, part // (TILE * GROUP)
    slot_ref[0] = 0
    slot = slot_ref[0]
    if both:
        vc, undo_c = leveled(x_ref[DIMS:, :], low)
        vc_ref[...] = halves(vc, BF16)
        vc_low_ref[...] = halves(vc, low)
        facc_ref[...] = jnp.zeros_like(facc_ref)
    vr, undo_r = leveled(jnp.concatenate([v[DIMS:, :] for v in vs], axis=1), low)
    vr_ref[...] = halves(vr, BF16)
    vr_low_ref[...] = halves(vr, low)
    acc_ref[...] = jnp.zeros_like(acc_ref)

    def distances(ref, group, j):
        first = group % per_part * TILE * GROUP
        rows = ats[group // per_part][first : first + TILE * GROUP, :]
        cols = jnp.concatenate([b_ref[2 * j], b_ref[2 * j + 1]], axis=1)
        ref[0] = jnp.maximum(dot(rows, cols, 1, 0), 1e-30)

    def products(hi, lo, i, j):
        rows, cols = slice(i * TILE, (i + 1) * TILE), slice(j * TILE, (j + 1) * TILE)
        acc_ref[:, cols] += dot(vr_ref[:, rows], hi, 1, 0) + dot(vr_low_ref[:, rows], lo, 1, 0)
        if both:
            facc_ref[:, rows] += dot(vc_ref[:, cols], hi, 1, 1) + dot(vc_low_ref[:, cols], lo, 1, 1)

    behind = None
    groups = [(i, j) for i in range(count * per_part) for j in range(across)]
    distances(even_ref, 0, 0)
    for t, (i, j) in enumerate(groups):
        now, later = (even_ref, odd_ref) if t % 2 == 0 else (odd_ref, even_ref)
        if t + 1 < len(groups):
            distances(later, *groups[t + 1])
        for g in range(GROUP):
            if behind is not None:
                products(*behind)
            hi, lo = kernel_tile(now[slot, g * TILE : (g + 1) * TILE, :], low)
            behind = hi, lo, i * GROUP + g, j
    products(*behind)
    bwd_ref[...] = fold(acc_ref[...], undo_r)
    if both:
        fwd_ref[...] = fold(facc_ref[...], undo_c)


VMEM = pl.BlockSpec(memory_space=pltpu.VMEM)
PARAMS = pltpu.CompilerParams(vmem_limit_bytes=40 * 2**20)


def first(x, inv):
    n = x.shape[1]
    return pl.pallas_call(
        first_kernel,
        out_shape=(
            jax.ShapeDtypeStruct((n, DEPTH), BF16),
            jax.ShapeDtypeStruct((n // 128, DEPTH, 128), BF16),
            jax.ShapeDtypeStruct((DIMS, 128), F32),
        ),
        in_specs=[VMEM, VMEM],
        out_specs=(VMEM, VMEM, VMEM),
        compiler_params=PARAMS,
        cost_estimate=pl.CostEstimate(flops=n * 64, bytes_accessed=n * 16, transcendentals=0),
        name="first",
    )(x, inv)


def prep(x, inv, rows):
    n = x.shape[1]
    return pl.pallas_call(
        rows_kernel if rows else cols_kernel,
        out_shape=jax.ShapeDtypeStruct((n, DEPTH) if rows else (n // 128, DEPTH, 128), BF16),
        in_specs=[VMEM, VMEM],
        out_specs=VMEM,
        compiler_params=PARAMS,
        cost_estimate=pl.CostEstimate(flops=n * 64, bytes_accessed=n * 16, transcendentals=0),
        name="rows" if rows else "cols",
    )(x, inv)


def tiles(ats, vs, b, x=None):
    n, width = len(ats) * ats[0].shape[0], b.shape[0] * 128
    both = x is not None
    low = F8 if both else BF16
    bwd = jax.ShapeDtypeStruct((RHS, width), F32)
    fwd = jax.ShapeDtypeStruct((RHS, n), F32)
    more = [
        pltpu.VMEM((2 * RHS, width), BF16),
        pltpu.VMEM((2 * RHS, width), low),
        pltpu.VMEM((2 * RHS, n), F32),
    ]
    return pl.pallas_call(
        functools.partial(tile_kernel, both, low, len(ats)),
        out_shape=(fwd, bwd) if both else bwd,
        in_specs=[VMEM] * (2 * len(ats) + (2 if both else 1)),
        out_specs=(VMEM, VMEM) if both else VMEM,
        scratch_shapes=(more if both else [])
        + [
            pltpu.VMEM((2 * RHS, n), BF16),
            pltpu.VMEM((2 * RHS, n), low),
            pltpu.VMEM((2 * RHS, width), F32),
            pltpu.VMEM((1, TILE * GROUP, TILE), F32),
            pltpu.VMEM((1, TILE * GROUP, TILE), F32),
            pltpu.SMEM((1,), jnp.int32),
        ],
        compiler_params=PARAMS,
        cost_estimate=pl.CostEstimate(
            flops=n * width * 8, bytes_accessed=n * 16, transcendentals=0
        ),
        name="both" if both else "own",
    )(*ats, *vs, b, *([x] if both else []))


def shifted(value, steps):
    count = lax.axis_size("blk")
    return lax.ppermute(value, "blk", [(s, (s + steps) % count) for s in range(count)])


def swapped(value, mask):
    count = lax.axis_size("split")
    return lax.ppermute(value, "split", [(s, s ^ mask) for s in range(count)])


def after(value, *others):
    return lax.optimization_barrier((value, *others))[0]


def body(points, vectors, inv_length, noise):
    row = lax.broadcasted_iota(jnp.int32, (DIMS + RHS, points.shape[1]), 0)
    own = jnp.where(row < DIMS, jnp.pad(points, ((0, RHS), (0, 0))), jnp.pad(vectors, ((DIMS, 0), (0, 0))))
    width = own.shape[1]
    near = swapped(own, 1)
    far = swapped(own, 2)
    two = shifted(own, 2)
    at0, b0, inv = first(own, inv_length.reshape(1, DIMS))
    total = tiles([at0], [own], b0)
    near = after(near, total)
    at_near = prep(near, inv, True)
    total = total + tiles([at_near], [near], b0)
    far = after(far, total)
    cross = swapped(far, 1)
    one = shifted(after(own, far), 1)
    at_far = prep(far, inv, True)
    b2 = prep(after(two, total), inv, False)
    cross = after(cross, b2)
    at_cross = prep(cross, inv, True)
    fwd2, ret2 = tiles([at0, at_far, at_cross, at_near], [own, far, cross, near], b2, two)
    back2 = shifted(ret2, -2)
    one = after(one, ret2)
    fwd1, ret1 = tiles([at0, at_far, at_cross, at_near], [own, far, cross, near], prep(one, inv, False), one)
    back1 = shifted(ret1, -1)
    fwd = fwd1 + fwd2
    give_near = swapped(fwd[:, 2 * width :], 1)
    rows_far = fwd[:, width : 2 * width] + give_near[:, :width]
    give_far = swapped(rows_far, 2)
    total = total + tiles([at_far, after(at_cross, rows_far)], [far, cross], b0)
    total = total + fwd[:, :width] + give_near[:, width:]
    return total + give_far + back1 + back2 + noise[None, :] * vectors


def solution(mesh):
    placed = (P(None, ("blk", "split")), P(None, ("blk", "split")), P(), P(("blk", "split")))
    return jax.shard_map(
        body, mesh=mesh, in_specs=placed, out_specs=P(None, ("blk", "split")), check_vma=False
    )
```

```python
import functools

import jax
import jax.numpy as jnp
from jax import lax
from jax.experimental import pallas as pl
from jax.experimental.pallas import tpu as pltpu
from jax.sharding import PartitionSpec as P

SIGNAL = 0.03125
ROOT_FIVE = 2.23606797749979
LOG2E = 1.4426950408889634
POINT_SCALE = ROOT_FIVE * LOG2E
OUT_SCALE = SIGNAL / (3.0 * LOG2E * LOG2E)
SHIFT = 1.5 * LOG2E
FLOOR = 0.75 * LOG2E * LOG2E
LIFT = 14.0
DIMS = 32
RHS = 16
DEPTH = 256
TILE = 256
GROUP = 2
BF16 = jnp.bfloat16
F32 = jnp.float32
F8 = jnp.float8_e4m3fn
PEAK = 128.0


def dot(a, b, ca, cb):
    return lax.dot_general(a, b, (((ca,), (cb,)), ((), ())), preferred_element_type=F32)


def pieces(x):
    hi = x.astype(BF16)
    rest = x - hi.astype(F32)
    mid = rest.astype(BF16)
    lo = (rest - mid.astype(F32)).astype(BF16)
    return hi, mid, lo


def norm_rows(sq, first):
    s1, s2, s3 = (p.astype(F32) for p in pieces(sq))
    row = lax.broadcasted_iota(jnp.int32, (16, sq.shape[1]), 0)
    out = jnp.where(row < 6, 1.0, 0.0)
    for k, s in enumerate((s1, s2, s3)):
        out = jnp.where(row == first + k, s, out)
    return out.astype(BF16)


def features(x, rows):
    sq = jnp.sum(x * x, axis=0, keepdims=True)
    hi, mid, lo = pieces(x)
    pad = jnp.zeros((DEPTH - 208, x.shape[1]), BF16)
    if rows:
        two = jnp.asarray(-2.0, BF16)
        hi, mid, lo = hi * two, mid * two, lo * two
        return jnp.concatenate([hi, mid, hi, lo, mid, hi, norm_rows(sq, 0), pad], axis=0)
    return jnp.concatenate([hi, hi, mid, hi, mid, lo, norm_rows(sq, 3), pad], axis=0)


def put_columns(b_ref, b):
    for k in range(b_ref.shape[0]):
        b_ref[k] = b[:, k * 128 : (k + 1) * 128]


def two_slabs(ref, k):
    return jnp.concatenate([ref[2 * k], ref[2 * k + 1]], axis=1)


def halves(v, kind):
    hi = v.astype(kind)
    return jnp.concatenate([hi, (v - hi.astype(F32)).astype(kind)], axis=0)


def kernel_tile(b2, low):
    if low == BF16:
        w = -SHIFT - b2 * lax.rsqrt(b2)
        t = (w * w + FLOOR) * jnp.exp2(w)
    else:
        b = b2 * lax.rsqrt(b2)
        t = ((b + 3.0 * LOG2E) * b + 3.0 * LOG2E * LOG2E) * jnp.exp2(LIFT - b)
    hi = t.astype(BF16)
    return hi, (t - hi.astype(F32)).astype(low)


def leveled(v, low):
    if low == BF16:
        return v, OUT_SCALE * 2.0**SHIFT
    top = jnp.maximum(jnp.max(jnp.abs(v), axis=1, keepdims=True), 1e-30)
    return v * (PEAK / top), top * (OUT_SCALE * 2.0**-LIFT / PEAK)


def fold(x, undo):
    return (x[:RHS] + x[RHS:]) * undo


def scaled(x_ref, inv):
    return (x_ref[:DIMS, :] * inv) * POINT_SCALE


def first_kernel(x_ref, inv_ref, at_ref, b_ref, inv_col_ref):
    row = lax.broadcasted_iota(jnp.int32, (DIMS, DIMS), 0)
    col = lax.broadcasted_iota(jnp.int32, (DIMS, DIMS), 1)
    inv = jnp.sum(jnp.where(row == col, inv_ref[...], 0.0), axis=1, keepdims=True)
    inv_col_ref[...] = jnp.broadcast_to(inv, inv_col_ref.shape)
    x = scaled(x_ref, inv)
    at_ref[...] = features(x, True).T
    put_columns(b_ref, features(x, False))


def rows_kernel(x_ref, inv_ref, at_ref):
    at_ref[...] = features(scaled(x_ref, inv_ref[:, :1]), True).T


def cols_kernel(x_ref, inv_ref, b_ref):
    put_columns(b_ref, features(scaled(x_ref, inv_ref[:, :1]), False))


def tile_kernel(both, low, count, *refs):
    ats, vs, b_ref, rest = refs[:count], refs[count : 2 * count], refs[2 * count], refs[2 * count + 1 :]
    if both:
        x_ref, fwd_ref, bwd_ref, vc_ref, vc_low_ref, facc_ref = rest[:6]
    else:
        bwd_ref = rest[0]
    vr_ref, vr_low_ref, acc_ref, even_ref, odd_ref, slot_ref = rest[6 if both else 1 :]
    part = ats[0].shape[0]
    across, per_part = b_ref.shape[0] * 128 // TILE, part // (TILE * GROUP)
    slot_ref[0] = 0
    slot = slot_ref[0]
    if both:
        vc, undo_c = leveled(x_ref[DIMS:, :], low)
        put_columns(vc_ref, halves(vc, BF16))
        put_columns(vc_low_ref, halves(vc, low))
        facc_ref[...] = jnp.zeros_like(facc_ref)
    vr, undo_r = leveled(jnp.concatenate([v[DIMS:, :] for v in vs], axis=1), low)
    put_columns(vr_ref, halves(vr, BF16))
    put_columns(vr_low_ref, halves(vr, low))
    acc_ref[...] = jnp.zeros_like(acc_ref)

    def distances(ref, group, j):
        first = group % per_part * TILE * GROUP
        rows = ats[group // per_part][first : first + TILE * GROUP, :]
        ref[0] = jnp.maximum(dot(rows, two_slabs(b_ref, j), 1, 0), 1e-30)

    def products(hi, lo, i, j):
        rows, cols = slice(i * TILE, (i + 1) * TILE), slice(j * TILE, (j + 1) * TILE)
        acc_ref[:, cols] += dot(two_slabs(vr_ref, i), hi, 1, 0) + dot(two_slabs(vr_low_ref, i), lo, 1, 0)
        if both:
            facc_ref[:, rows] += dot(two_slabs(vc_ref, j), hi, 1, 1) + dot(two_slabs(vc_low_ref, j), lo, 1, 1)

    behind = None
    groups = [(i, j) for i in range(count * per_part) for j in range(across)]
    distances(even_ref, 0, 0)
    for t, (i, j) in enumerate(groups):
        now, later = (even_ref, odd_ref) if t % 2 == 0 else (odd_ref, even_ref)
        if t + 1 < len(groups):
            distances(later, *groups[t + 1])
        for g in range(GROUP):
            if behind is not None:
                products(*behind)
            hi, lo = kernel_tile(now[slot, g * TILE : (g + 1) * TILE, :], low)
            behind = hi, lo, i * GROUP + g, j
    products(*behind)
    bwd_ref[...] = fold(acc_ref[...], undo_r)
    if both:
        fwd_ref[...] = fold(facc_ref[...], undo_c)


VMEM = pl.BlockSpec(memory_space=pltpu.VMEM)
PARAMS = pltpu.CompilerParams(vmem_limit_bytes=40 * 2**20)


def first(x, inv):
    n = x.shape[1]
    return pl.pallas_call(
        first_kernel,
        out_shape=(
            jax.ShapeDtypeStruct((n, DEPTH), BF16),
            jax.ShapeDtypeStruct((n // 128, DEPTH, 128), BF16),
            jax.ShapeDtypeStruct((DIMS, 128), F32),
        ),
        in_specs=[VMEM, VMEM],
        out_specs=(VMEM, VMEM, VMEM),
        compiler_params=PARAMS,
        cost_estimate=pl.CostEstimate(flops=n * 64, bytes_accessed=n * 16, transcendentals=0),
        name="first",
    )(x, inv)


def prep(x, inv, rows):
    n = x.shape[1]
    return pl.pallas_call(
        rows_kernel if rows else cols_kernel,
        out_shape=jax.ShapeDtypeStruct((n, DEPTH) if rows else (n // 128, DEPTH, 128), BF16),
        in_specs=[VMEM, VMEM],
        out_specs=VMEM,
        compiler_params=PARAMS,
        cost_estimate=pl.CostEstimate(flops=n * 64, bytes_accessed=n * 16, transcendentals=0),
        name="rows" if rows else "cols",
    )(x, inv)


def tiles(ats, vs, b, x=None):
    n, width = len(ats) * ats[0].shape[0], b.shape[0] * 128
    both = x is not None
    low = F8 if both else BF16
    bwd = jax.ShapeDtypeStruct((RHS, width), F32)
    fwd = jax.ShapeDtypeStruct((RHS, n), F32)
    more = [
        pltpu.VMEM((width // 128, 2 * RHS, 128), BF16),
        pltpu.VMEM((width // 128, 2 * RHS, 128), low),
        pltpu.VMEM((2 * RHS, n), F32),
    ]
    return pl.pallas_call(
        functools.partial(tile_kernel, both, low, len(ats)),
        out_shape=(fwd, bwd) if both else bwd,
        in_specs=[VMEM] * (2 * len(ats) + (2 if both else 1)),
        out_specs=(VMEM, VMEM) if both else VMEM,
        scratch_shapes=(more if both else [])
        + [
            pltpu.VMEM((n // 128, 2 * RHS, 128), BF16),
            pltpu.VMEM((n // 128, 2 * RHS, 128), low),
            pltpu.VMEM((2 * RHS, width), F32),
            pltpu.VMEM((1, TILE * GROUP, TILE), F32),
            pltpu.VMEM((1, TILE * GROUP, TILE), F32),
            pltpu.SMEM((1,), jnp.int32),
        ],
        compiler_params=PARAMS,
        cost_estimate=pl.CostEstimate(
            flops=n * width * 8, bytes_accessed=n * 16, transcendentals=0
        ),
        name="both" if both else "own",
    )(*ats, *vs, b, *([x] if both else []))


def shifted(value, steps):
    count = lax.axis_size("blk")
    return lax.ppermute(value, "blk", [(s, (s + steps) % count) for s in range(count)])


def swapped(value, mask):
    count = lax.axis_size("split")
    return lax.ppermute(value, "split", [(s, s ^ mask) for s in range(count)])


def after(value, *others):
    return lax.optimization_barrier((value, *others))[0]


def body(points, vectors, inv_length, noise):
    row = lax.broadcasted_iota(jnp.int32, (DIMS + RHS, points.shape[1]), 0)
    own = jnp.where(row < DIMS, jnp.pad(points, ((0, RHS), (0, 0))), jnp.pad(vectors, ((DIMS, 0), (0, 0))))
    width = own.shape[1]
    near = swapped(own, 1)
    far = swapped(own, 2)
    two = shifted(own, 2)
    at0, b0, inv = first(own, inv_length.reshape(1, DIMS))
    total = tiles([at0], [own], b0)
    near = after(near, total)
    at_near = prep(near, inv, True)
    total = total + tiles([at_near], [near], b0)
    far = after(far, total)
    cross = swapped(far, 1)
    one = shifted(after(own, far), 1)
    at_far = prep(far, inv, True)
    b2 = prep(after(two, total), inv, False)
    cross = after(cross, b2)
    at_cross = prep(cross, inv, True)
    fwd2, ret2 = tiles([at0, at_far, at_cross, at_near], [own, far, cross, near], b2, two)
    back2 = shifted(ret2, -2)
    one = after(one, ret2)
    fwd1, ret1 = tiles([at0, at_far, at_cross, at_near], [own, far, cross, near], prep(one, inv, False), one)
    back1 = shifted(ret1, -1)
    fwd = fwd1 + fwd2
    give_near = swapped(fwd[:, 2 * width :], 1)
    rows_far = fwd[:, width : 2 * width] + give_near[:, :width]
    give_far = swapped(rows_far, 2)
    total = total + tiles([at_far, after(at_cross, rows_far)], [far, cross], b0)
    total = total + fwd[:, :width] + give_near[:, width:]
    return total + give_far + back1 + back2 + noise[None, :] * vectors


def solution(mesh):
    placed = (P(None, ("blk", "split")), P(None, ("blk", "split")), P(), P(("blk", "split")))
    return jax.shard_map(
        body, mesh=mesh, in_specs=placed, out_specs=P(None, ("blk", "split")), check_vma=False
    )
```
